32 devices in a mesh: tile: 8 (over y, x, core), lev: 4 (over z).
Axes of the slice: x: 2, y: 2, z: 4, core: 2. Of those that a mesh axis runs over, the one named last changes fastest.
Arguments:
- tracer: float32 [2, 72, 16, 512], P(None, 'lev', 'tile'), may hold values from -6 to 6
- u_courant: float32 [72, 16, 512], P('lev', 'tile'), may hold values from -0.45 to 0.45
- v_courant: float32 [72, 16, 512], P('lev', 'tile'), may hold values from -0.45 to 0.45
- surface_flux: float32 [2, 16, 512], P(None, 'tile'), may hold values from -6 to 6
- mixing: float32 [72, 72], replicated, may hold values from 0 to 1
- kernel: float32 [72, 32768], P('lev', 'tile'), may hold values from 0.1 to 1
- column: int32 [32768], P('tile'), may hold values from 0 to 1023
- owner_tile: int32 [32768], P('tile'), may hold values from 0 to 7, as said below
- offset: int32 [32768], P('tile'), may hold values from 0 to 23
- counts: int32 [8], P('tile'), may hold values from 2048 to 4096, as said below
Outputs:
- transported: float32 [2, 72, 16, 512], P(None, 'lev', 'tile')
- evolved: float32 [2, 32768], P(None, 'tile')
The draws below stay inside these ranges and needn't reach their ends.
Inputs may be any that keep to these rules, and one draw needn't show every extreme that they name: `owner_tile`: among the rows of one device, no owner tile is named by more than 1536 rows; one owner tile, the same for every device, is named by exactly 1536 rows of each device. Rows at position counts[t] and beyond in tile t's block of soundings are unused.
All inputs are finite; a program needn't handle non-finite values.
Results may differ from the reference program's by a relative error of at most 0.0003.
Values sent between devices are 32-bit elements; how exact they have to be, the bound alone decides.
A program may use at most 64 MiB of HBM per device.

```python
import math
import jax
import jax.numpy as jnp
from jax import lax

SCEN = 2
NLEV = 72
LON_DEV = 2
NLAT = 512
NSUB = 2
SND_DEV = 4096
TILES = 8
NLON = 16
SND_TOTAL = 32768
CAP = 1536


def draw_mixing(key, part):
    level_ids = jnp.arange(NLEV)
    identity_mask = (level_ids[:, None] == level_ids[None, :]).astype(jnp.float32)
    spread = jax.random.uniform(key, (NLEV, NLEV), jnp.float32)
    return 0.6 * identity_mask + 0.8 / NLEV * spread * (1.0 - identity_mask)


def draw_owner_tile(key, part):
    hot_owner = jax.random.randint(jax.random.fold_in(key, 1), (), 0, TILES)
    remaining = SND_DEV - CAP

    def one_block(block_key):
        first_key, second_key = jax.random.split(block_key)
        chosen = jax.random.permutation(first_key, (TILES - 1) * CAP)[:remaining]
        others = (hot_owner + 1 + chosen // CAP) % TILES
        owners = jnp.concatenate([jnp.full((CAP,), hot_owner, jnp.int32), others.astype(jnp.int32)])
        shuffle = jax.random.permutation(second_key, SND_DEV)
        return owners[shuffle]
    block_keys = jax.random.split(jax.random.fold_in(key, 2), TILES)
    return jax.vmap(one_block)(block_keys).reshape(-1).astype(jnp.int32)


def draw_counts(key, part):
    drawn = jax.random.randint(jax.random.fold_in(key, 3), (TILES,), SND_DEV // 2, SND_DEV + 1)
    full_tile = jax.random.randint(jax.random.fold_in(key, 4), (), 0, TILES)
    tile_ids = jnp.arange(TILES)
    return jnp.where(tile_ids == full_tile, SND_DEV, drawn).astype(jnp.int32)


def set_ends(values, stream_key, smallest, top_value):
    index_at = [jax.random.randint(jax.random.fold_in(stream_key, axis), (), 0, length) for axis, length in enumerate(values.shape)]
    widest = values.shape.index(max(values.shape))
    beside = index_at[:widest] + [(index_at[widest] + 1) % values.shape[widest]] + index_at[widest + 1:]
    return values.at[tuple(index_at)].set(smallest).at[tuple(beside)].set(top_value)


def steps_of(own_key, extent, pieces, least, high):
    def one(position, blocks):
        heights = jax.random.uniform(jax.random.fold_in(jax.random.fold_in(own_key, 6), position), (blocks,), jnp.float32, least / len(pieces), high / len(pieces))
        return jnp.repeat(jnp.exp(heights), extent[position] // blocks).reshape((-1,) + (1,) * (len(extent) - position - 1))

    level = one(*pieces[0])
    for cut in pieces[1:]:
        level = level * one(*cut)
    return level


def centred(own_key, shape, scale, bound, pieces=(), kind=jnp.bfloat16):
    array = scale * jax.random.normal(own_key, shape, jnp.float32)
    if pieces:
        array = array * steps_of(own_key, shape, pieces, -0.22, 0.18)
    return jnp.clip(array, -bound, bound).astype(kind)


def setup_inputs(seed: int = 0) -> dict:
    seeds = jax.random.split(jax.random.key(seed), 11)
    tracer = centred(seeds[0], (SCEN, NLEV, NLON, NLAT), 1.0, 6.0, ((1, 4), (2, 8)), jnp.float32)
    u_courant = jnp.clip(jax.random.uniform(seeds[1], (NLEV, NLON, NLAT), jnp.float32, -0.45, 0.45) * steps_of(seeds[1], (NLEV, NLON, NLAT), ((0, 4), (1, 8)), -0.4, 0.0), -0.45, 0.45)
    v_courant = jnp.clip(jax.random.uniform(seeds[2], (NLEV, NLON, NLAT), jnp.float32, -0.45, 0.45) * steps_of(seeds[2], (NLEV, NLON, NLAT), ((0, 4), (1, 8)), -0.4, 0.0), -0.45, 0.45)
    surface_flux = centred(seeds[3], (SCEN, NLON, NLAT), 1.0, 6.0, ((1, 8),), jnp.float32)
    mixing = draw_mixing(jax.random.fold_in(seeds[10], 71), 0)
    kernel = jnp.clip(jnp.exp(math.log(1.0) - 2.3025851 * jax.random.uniform(seeds[5], (NLEV, SND_TOTAL), jnp.float32) ** steps_of(seeds[5], (NLEV, SND_TOTAL), ((0, 4), (1, 8)), -0.2, 0.2)), 0.1, 1.0)
    column = set_ends(jax.random.randint(seeds[6], (SND_TOTAL,), 0, LON_DEV * NLAT), jax.random.fold_in(seeds[6], 1), 0, (LON_DEV * NLAT) - 1).astype(jnp.int32)
    owner_tile = draw_owner_tile(jax.random.fold_in(seeds[10], 71), 0)
    offset = set_ends(jax.random.randint(seeds[8], (SND_TOTAL,), 0, NLEV // 3), jax.random.fold_in(seeds[8], 1), 0, (NLEV // 3) - 1).astype(jnp.int32)
    counts = draw_counts(jax.random.fold_in(seeds[10], 71), 0)
    return {"tracer": tracer, "u_courant": u_courant, "v_courant": v_courant, "surface_flux": surface_flux, "mixing": mixing, "kernel": kernel, "column": column, "owner_tile": owner_tile, "offset": offset, "counts": counts}


def substep(extended, wind_u, wind_v):
    centre = extended[:, :, 1:-1]
    west_cells = extended[:, :, :-2]
    east_cells = extended[:, :, 2:]
    wind_west = wind_u[:, 1:-1]
    wind_east = wind_u[:, 2:]
    wind_lat = wind_v[:, 1:-1]
    flux_west = wind_west * jnp.where(wind_west > 0, west_cells, centre)
    flux_east = wind_east * jnp.where(wind_east > 0, centre, east_cells)
    south_cells = jnp.concatenate([jnp.zeros_like(centre[..., :1]), centre[..., :-1]], axis=-1)
    lat_ids = lax.broadcasted_iota(jnp.int32, wind_lat.shape, 2)
    open_face = jnp.where(lat_ids > 0, wind_lat, jnp.zeros_like(wind_lat))
    flux_south = open_face * jnp.where(wind_lat > 0, south_cells, centre)
    flux_north = jnp.concatenate([flux_south[..., 1:], jnp.zeros_like(flux_south[..., :1])], axis=-1)
    return centre - (flux_east - flux_west) - (flux_north - flux_south)


def reference(tracer, u_courant, v_courant, surface_flux, mixing, kernel, column, owner_tile, offset, counts):
    advected = tracer.at[:, 0].add(surface_flux)
    winds_u = jnp.concatenate([u_courant[:, -1:], u_courant, u_courant[:, :1]], axis=1)
    winds_v = jnp.concatenate([v_courant[:, -1:], v_courant, v_courant[:, :1]], axis=1)
    for sub_step in range(NSUB):
        extended = jnp.concatenate([advected[:, :, -1:], advected, advected[:, :, :1]], axis=2)
        advected = substep(extended, winds_u, winds_v)
    transported = jnp.einsum("kl,slxy->skxy", mixing, advected, precision=lax.Precision.HIGHEST)
    columns_flat = transported.reshape(SCEN, NLEV, TILES, LON_DEV * NLAT)
    picked = columns_flat[:, :, owner_tile, column]
    level_ids = jnp.arange(NLEV, dtype=jnp.int32)[:, None]
    weighted = jnp.where(level_ids >= offset[None, :], kernel, jnp.zeros_like(kernel))
    sampled = jnp.sum(picked * weighted[None], axis=1)
    denominator = jnp.sum(weighted, axis=0)
    positions = jnp.arange(SND_TOTAL, dtype=jnp.int32)
    in_use = (positions % SND_DEV) < counts[positions // SND_DEV]
    evolved = jnp.where(in_use[None, :], sampled / denominator[None, :], jnp.zeros_like(sampled))
    return transported, evolved
```

```python
import functools
import jax
import jax.numpy as jnp
from jax import lax
from jax.experimental import pallas as pl
from jax.experimental.pallas import tpu as pltpu
from jax.sharding import PartitionSpec as P

NSUB = 2
PAD = 24
KPAD = 32
NB = 256
GROUP = 8
MESH = pl.DeviceIdType.MESH


def split(x):
    high = x.astype(jnp.bfloat16)
    low = (x - high.astype(jnp.float32)).astype(jnp.bfloat16)
    return high, low


def flip(index, bit):
    return index + bit - 2 * bit * ((index // bit) % 2)


def substep(cells, winds, lat_winds, lat_ids):
    count = len(lat_winds)
    size = cells[0].shape[-1]
    west = [
        winds[i] * jnp.where(winds[i] > 0, cells[i], cells[i + 1]) for i in range(count + 1)
    ]
    result = []
    for i in range(count):
        centre = cells[i + 1]
        south_cells = pltpu.roll(centre, 1, 1)
        south = lat_winds[i] * jnp.where(lat_winds[i] > 0, south_cells, centre)
        south = jnp.where(lat_ids > 0, south, 0.0)
        north = pltpu.roll(south, size - 1, 1)
        result.append(centre - (west[i + 1] - west[i]) - (north - south))
    return result


def kernel_body(
    dims,
    tracer, u_ref, v_ref, flux, mix, kern, column, owner, offset, counts,
    out, evolved,
    cur, halo_w, halo_e, halo_u, levs, rhs, gathered, lhs, onehot, lon_of, weight,
    nums, dens, pad,
    h_send, h_recv, u_sem, z_send, z_recv, g_send, g_recv, n_send, n_recv,
):
    scen, lev_here, lon_here, nlat, snd, tiles, nlev = dims
    me, lev = lax.axis_index("tile"), lax.axis_index("lev")
    east, west = lax.rem(me + 1, tiles), lax.rem(me + tiles - 1, tiles)
    bits = [1 << k for k in range(tiles.bit_length() - 1)]
    peers = [lax.rem(lev + r, nlev) for r in range(1, nlev)]

    barrier = pltpu.get_barrier_semaphore()
    friends = [(east, lev), (west, lev)]
    friends += [(flip(me, b), lev) for b in bits]
    friends += [(me, p) for p in peers]
    for friend in friends:
        pl.semaphore_signal(barrier, inc=1, device_id=friend, device_id_type=MESH)

    row_ids = lax.broadcasted_iota(jnp.int32, (lev_here, nlat), 0)
    lat_ids = lax.broadcasted_iota(jnp.int32, (lev_here, nlat), 1)
    bottom = jnp.logical_and(row_ids == 0, lev == 0)
    for s in range(scen):
        for i in range(lon_here):
            here = tracer[s, i]
            cur[0, s, i] = jnp.where(bottom, here + flux[s, pl.ds(i, 1)], here)
    pl.semaphore_wait(barrier, len(friends))

    def remote(src, dst, send, recv, device):
        return pltpu.make_async_remote_copy(
            src_ref=src, dst_ref=dst, send_sem=send, recv_sem=recv,
            device_id=device, device_id_type=MESH,
        )

    pending = []

    def send_halo(step, s):
        to_east = remote(
            cur.at[step, s, lon_here - 1], halo_w.at[step, s],
            h_send.at[step, s, 0], h_recv.at[step, s, 0], (east, lev),
        )
        to_west = remote(
            cur.at[step, s, 0], halo_e.at[step, s],
            h_send.at[step, s, 1], h_recv.at[step, s, 1], (west, lev),
        )
        to_east.start()
        to_west.start()
        pending.extend([to_east, to_west])
        return to_east, to_west

    u_copy = remote(u_ref.at[0], halo_u, u_sem.at[0], u_sem.at[1], (west, lev))
    u_copy.start()
    pending.append(u_copy)
    halos = {(0, s): send_halo(0, s) for s in range(scen)}

    level_ids = lev * lev_here + lax.broadcasted_iota(jnp.int32, (lev_here, NB), 0)
    lat_rows = lax.broadcasted_iota(jnp.int32, (nlat, NB), 0)

    def prepare(nb, carry):
        at = pl.ds(pl.multiple_of(nb * NB, NB), NB)
        col = column[:, at]
        lon_in = col // nlat
        lat = col - lon_in * nlat
        onehot[:, at] = (lat_rows == lat).astype(jnp.float32).astype(jnp.bfloat16)
        lon_of[:, at] = owner[:, at] * lon_here + lon_in
        used_weight = jnp.where(level_ids >= offset[:, at], kern[:, at], 0.0)
        weight[:, at] = used_weight
        dens[lev, :, at] = jnp.sum(used_weight, axis=0, keepdims=True)
        return carry

    lax.fori_loop(0, snd // NB, prepare, 0)
    pad[...] = jnp.zeros_like(pad)

    u_copy.wait_recv()
    for step in range(NSUB):
        for s in range(scen):
            for copy in halos[(step, s)]:
                copy.wait_recv()
            cells = [halo_w[step, s]] + [cur[step, s, i] for i in range(lon_here)]
            cells.append(halo_e[step, s])
            winds = [u_ref[i] for i in range(lon_here)] + [halo_u[...]]
            new = substep(cells, winds, [v_ref[i] for i in range(lon_here)], lat_ids)
            if step < NSUB - 1:
                for i in range(lon_here):
                    cur[step + 1, s, i] = new[i]
                halos[(step + 1, s)] = send_halo(step + 1, s)
            else:
                for i in range(lon_here):
                    levs[s, lev, i] = new[i]
                copies = []
                for r, peer in enumerate(peers):
                    copy = remote(
                        levs.at[s, lev], levs.at[s, lev],
                        z_send.at[s, r], z_recv.at[s, r], (me, peer),
                    )
                    copy.start()
                    copies.append(copy)
                pending.extend(copies)
                halos[("z", s)] = copies

    den_copies = []
    for r, peer in enumerate(peers):
        copy = remote(
            dens.at[lev], dens.at[lev],
            n_send.at[scen, r], n_recv.at[scen, r], (me, peer),
        )
        copy.start()
        den_copies.append(copy)

    routes = {}
    for s in range(scen):
        for copy in halos[("z", s)]:
            copy.wait_recv()
        for i in range(lon_here):
            for z in range(nlev):
                pad[0:lev_here] = levs[s, z, i]
                high, low = split(pad[...])
                rhs[z * KPAD:(z + 1) * KPAD] = high
                rhs[(nlev + z) * KPAD:(nlev + z + 1) * KPAD] = low
            both = jnp.dot(mix[...], rhs[...], preferred_element_type=jnp.float32)
            total = both[0:PAD] + both[PAD:2 * PAD]
            gathered[s, 0, i] = total[0:lev_here]
            out[s, i] = total[0:lev_here]
        order = bits[::-1] if s % 2 == 0 else bits[-2::-1][:-1] + [bits[-1]] + bits[:1]
        held, sent = [0], []
        routes[s] = []
        for bit in order:
            step_copies = []
            for m in held:
                copy = remote(
                    gathered.at[s, m], gathered.at[s, m + bit],
                    g_send.at[s, m + bit], g_recv.at[s, m + bit], (flip(me, bit), lev),
                )
                step_copies.append((m, copy))
            routes[s].append(step_copies)
            held = held + [m + bit for m in held]
    for s in range(scen):
        for _, copy in routes[s][0]:
            copy.start()
    for k in range(1, len(bits)):
        for s in range(scen):
            for _, copy in routes[s][k - 1]:
                copy.wait_recv()
            for _, copy in routes[s][k]:
                copy.start()

    rows = GROUP * lon_here * PAD
    for s in range(scen):
        for _, copy in routes[s][-1]:
            copy.wait_recv()
        for m in range(tiles):
            group, inner = m // GROUP, m % GROUP
            for i in range(lon_here):
                pad[0:lev_here] = gathered[s, m, i]
                value = pad[0:PAD] if i == 0 else jnp.concatenate([value, pad[0:PAD]], axis=0)
            high, low = split(value)
            at = inner * lon_here * PAD
            lhs[group, at:at + lon_here * PAD] = high
            lhs[group, rows + at:rows + at + lon_here * PAD] = low

        def sample(nb, carry):
            at = pl.ds(pl.multiple_of(nb * NB, NB), NB)
            hot = onehot[:, at]
            lon_ids = jnp.broadcast_to(lon_of[:, at], (PAD, NB))

            def one_group(group, acc):
                found = jnp.dot(lhs[group], hot, preferred_element_type=jnp.float32)
                for inner in range(GROUP):
                    tile = jnp.bitwise_xor(me, group * GROUP + inner)
                    for i in range(lon_here):
                        r = (inner * lon_here + i) * PAD
                        block = found[r:r + PAD] + found[rows + r:rows + r + PAD]
                        acc = jnp.where(lon_ids == tile * lon_here + i, block, acc)
                return acc

            acc = jnp.zeros((PAD, NB), jnp.float32)
            if tiles == GROUP:
                acc = one_group(0, acc)
            else:
                acc = lax.fori_loop(0, tiles // GROUP, one_group, acc)
            terms = acc[0:lev_here] * weight[:, at]
            nums[s, lev, :, at] = jnp.sum(terms, axis=0, keepdims=True)
            return carry

        lax.fori_loop(0, snd // NB, sample, 0)
        copies = []
        for r, peer in enumerate(peers):
            copy = remote(
                nums.at[s, lev], nums.at[s, lev],
                n_send.at[s, r], n_recv.at[s, r], (me, peer),
            )
            copy.start()
            copies.append(copy)
        halos[("n", s)] = copies

    for copy in den_copies:
        copy.wait_recv()
    den = dens[0]
    for z in range(1, nlev):
        den = den + dens[z]
    in_use = lax.broadcasted_iota(jnp.int32, (1, snd), 1) < counts[0]
    for s in range(scen):
        for copy in halos[("n", s)]:
            copy.wait_recv()
        num = nums[s, 0]
        for z in range(1, nlev):
            num = num + nums[s, z]
        evolved[s] = jnp.where(in_use, num / den, 0.0)
        pending.extend(halos[("n", s)])
    pending.extend(den_copies)
    for s in range(scen):
        for step_copies in routes[s]:
            pending.extend(copy for _, copy in step_copies)
    for copy in pending:
        copy.wait_send()


def body(
    tracer, u_courant, v_courant, surface_flux, mixing, kernel, column, owner_tile, offset, counts
):
    scen, lev_here, lon_here, nlat = tracer.shape
    snd = column.shape[0]
    tiles, nlev = lax.axis_size("tile"), lax.axis_size("lev")
    lev = lax.axis_index("lev")
    rows = lax.dynamic_slice_in_dim(mixing, lev * lev_here, lev_here, 0)
    rows = rows.reshape(lev_here, nlev, lev_here)
    rows = jnp.pad(rows, ((0, PAD - lev_here), (0, 0), (0, KPAD - lev_here)))
    rows = rows.reshape(PAD, nlev * KPAD)
    high = lax.reduce_precision(rows, 8, 7)
    low = rows - high
    mix = jnp.concatenate(
        [
            jnp.concatenate([high, high], axis=1),
            jnp.concatenate([low, jnp.zeros_like(low)], axis=1),
        ],
        axis=0,
    ).astype(jnp.bfloat16)
    f32, bf16 = jnp.float32, jnp.bfloat16
    block = (lev_here, nlat)
    dma = pltpu.SemaphoreType.DMA
    vmem = pl.BlockSpec(memory_space=pltpu.VMEM)
    groups = tiles // GROUP
    out, evolved = pl.pallas_call(
        functools.partial(kernel_body, (scen, lev_here, lon_here, nlat, snd, tiles, nlev)),
        out_shape=(
            jax.ShapeDtypeStruct((scen, lon_here) + block, f32),
            jax.ShapeDtypeStruct((scen, 1, snd), f32),
        ),
        in_specs=[vmem] * 9 + [pl.BlockSpec(memory_space=pltpu.SMEM)],
        out_specs=(vmem, vmem),
        scratch_shapes=[
            pltpu.VMEM((NSUB, scen, lon_here) + block, f32),
            pltpu.VMEM((NSUB, scen) + block, f32),
            pltpu.VMEM((NSUB, scen) + block, f32),
            pltpu.VMEM(block, f32),
            pltpu.VMEM((scen, nlev, lon_here) + block, f32),
            pltpu.VMEM((2 * nlev * KPAD, nlat), bf16),
            pltpu.VMEM((scen, tiles, lon_here) + block, f32),
            pltpu.VMEM((groups, 2 * GROUP * lon_here * PAD, nlat), bf16),
            pltpu.VMEM((nlat, snd), bf16),
            pltpu.VMEM((1, snd), jnp.int32),
            pltpu.VMEM((lev_here, snd), f32),
            pltpu.VMEM((scen, nlev, 1, snd), f32),
            pltpu.VMEM((nlev, 1, snd), f32),
            pltpu.VMEM((KPAD, nlat), f32),
            dma((NSUB, scen, 2)),
            dma((NSUB, scen, 2)),
            dma((2,)),
            dma((scen, nlev - 1)),
            dma((scen, nlev - 1)),
            dma((scen, tiles)),
            dma((scen, tiles)),
            dma((scen + 1, nlev - 1)),
            dma((scen + 1, nlev - 1)),
        ],
        compiler_params=pltpu.CompilerParams(
            collective_id=0, has_side_effects=True, vmem_limit_bytes=56 * 2**20
        ),
    )(
        tracer.transpose(0, 2, 1, 3),
        u_courant.transpose(1, 0, 2),
        v_courant.transpose(1, 0, 2),
        surface_flux,
        mix,
        kernel,
        column[None],
        owner_tile[None],
        offset[None],
        counts,
    )
    return out.transpose(0, 2, 1, 3), evolved[:, 0]


def solution(mesh):
    in_specs = (
        P(None, "lev", "tile", None),
        P("lev", "tile", None),
        P("lev", "tile", None),
        P(None, "tile", None),
        P(),
        P("lev", "tile"),
        P("tile"),
        P("tile"),
        P("tile"),
        P("tile"),
    )
    out_specs = (P(None, "lev", "tile", None), P(None, "tile"))
    return jax.shard_map(body, mesh=mesh, in_specs=in_specs, out_specs=out_specs, check_vma=False)
```

```python
import functools
import jax
import jax.numpy as jnp
from jax import lax
from jax.experimental import pallas as pl
from jax.experimental.pallas import tpu as pltpu
from jax.sharding import PartitionSpec as P

NSUB = 2
PAD = 24
KPAD = 32
NB = 256
GROUP = 8
MESH = pl.DeviceIdType.MESH


def split(x):
    high = x.astype(jnp.bfloat16)
    low = (x - high.astype(jnp.float32)).astype(jnp.bfloat16)
    return high, low


def flip(index, bit):
    return index + bit - 2 * bit * ((index // bit) % 2)


def substep(cells, winds, lat_winds, lat_ids):
    count = len(lat_winds)
    size = cells[0].shape[-1]
    west = [
        winds[i] * jnp.where(winds[i] > 0, cells[i], cells[i + 1]) for i in range(count + 1)
    ]
    result = []
    for i in range(count):
        centre = cells[i + 1]
        south_cells = pltpu.roll(centre, 1, 1)
        south = lat_winds[i] * jnp.where(lat_winds[i] > 0, south_cells, centre)
        south = jnp.where(lat_ids > 0, south, 0.0)
        north = pltpu.roll(south, size - 1, 1)
        result.append(centre - (west[i + 1] - west[i]) - (north - south))
    return result


def kernel_body(
    dims,
    tracer, u_ref, v_ref, flux, mix, kern, column, owner, offset, counts,
    out, evolved,
    cur, halo_w, halo_e, halo_u, levs, mixed, rhs, gathered, lhs, onehot, lon_of, weight,
    nums, dens, pad,
    h_send, h_recv, u_sem, z_send, z_recv, g_send, g_recv, n_send, n_recv, d_send, d_recv,
):
    scen, lev_here, lon_here, nlat, snd, tiles, nlev = dims
    me, lev = lax.axis_index("tile"), lax.axis_index("lev")
    east, west = lax.rem(me + 1, tiles), lax.rem(me + tiles - 1, tiles)
    bits = [1 << k for k in range(tiles.bit_length() - 1)]
    peers = [lax.rem(lev + r, nlev) for r in range(1, nlev)]

    barrier = pltpu.get_barrier_semaphore()
    friends = [(east, lev), (west, lev)]
    friends += [(flip(me, b), lev) for b in bits]
    friends += [(me, p) for p in peers]
    for friend in friends:
        pl.semaphore_signal(barrier, inc=1, device_id=friend, device_id_type=MESH)

    row_ids = lax.broadcasted_iota(jnp.int32, (lev_here, nlat), 0)
    lat_ids = lax.broadcasted_iota(jnp.int32, (lev_here, nlat), 1)
    bottom = jnp.logical_and(row_ids == 0, lev == 0)
    for s in range(scen):
        for i in range(lon_here):
            here = tracer[s, i]
            cur[0, s, i] = jnp.where(bottom, here + flux[s, pl.ds(i, 1)], here)
    pl.semaphore_wait(barrier, len(friends))

    def remote(src, dst, send, recv, device):
        return pltpu.make_async_remote_copy(
            src_ref=src, dst_ref=dst, send_sem=send, recv_sem=recv,
            device_id=device, device_id_type=MESH,
        )

    pending = []

    def send_halo(step, s):
        to_east = remote(
            cur.at[step, s, lon_here - 1], halo_w.at[step, s],
            h_send.at[step, s, 0], h_recv.at[step, s, 0], (east, lev),
        )
        to_west = remote(
            cur.at[step, s, 0], halo_e.at[step, s],
            h_send.at[step, s, 1], h_recv.at[step, s, 1], (west, lev),
        )
        to_east.start()
        to_west.start()
        pending.extend([to_east, to_west])
        return to_east, to_west

    u_copy = remote(u_ref.at[0], halo_u, u_sem.at[0], u_sem.at[1], (west, lev))
    u_copy.start()
    pending.append(u_copy)
    halos = {(0, s): send_halo(0, s) for s in range(scen)}

    level_ids = lev * lev_here + lax.broadcasted_iota(jnp.int32, (lev_here, NB), 0)
    lat_rows = lax.broadcasted_iota(jnp.int32, (nlat, NB), 0)
    steps = snd // NB

    def prepare(nb, carry):
        at = pl.ds(pl.multiple_of(nb * NB, NB), NB)
        col = column[:, at]
        lon_in = col // nlat
        lat = col - lon_in * nlat
        onehot[:, at] = (lat_rows == lat).astype(jnp.float32).astype(jnp.bfloat16)
        lon_of[:, at] = owner[:, at] * lon_here + lon_in
        used_weight = jnp.where(level_ids >= offset[:, at], kern[:, at], 0.0)
        weight[:, at] = used_weight
        dens[lev, :, at] = jnp.sum(used_weight, axis=0, keepdims=True)
        return carry

    lax.fori_loop(0, steps // 2, prepare, 0)
    pad[...] = jnp.zeros_like(pad)

    half, parity = lev // 2, lev % 2
    is_end = half == parity
    mate = half * 2 + 1 - parity

    def z_copy(s, k, src, dst, to):
        return remote(src, dst, z_send.at[s, k], z_recv.at[s, k], (me, to))

    def raw_copy(s, k, to):
        return z_copy(s, k, levs.at[s, lev], levs.at[s, lev], to)

    def mixed_copy(s):
        return z_copy(s, 3, mixed.at[s], gathered.at[s, 0], mate)

    u_copy.wait_recv()
    for step in range(NSUB):
        for s in range(scen):
            for copy in halos[(step, s)]:
                copy.wait_recv()
            cells = [halo_w[step, s]] + [cur[step, s, i] for i in range(lon_here)]
            cells.append(halo_e[step, s])
            winds = [u_ref[i] for i in range(lon_here)] + [halo_u[...]]
            new = substep(cells, winds, [v_ref[i] for i in range(lon_here)], lat_ids)
            if step < NSUB - 1:
                for i in range(lon_here):
                    cur[step + 1, s, i] = new[i]
                halos[(step + 1, s)] = send_halo(step + 1, s)
            else:
                for i in range(lon_here):
                    levs[s, lev, i] = new[i]

                @pl.when(is_end)
                def _():
                    raw_copy(s, 2, nlev - 1 - mate).start()
                    raw_copy(s, 0, mate).start()

                @pl.when(jnp.logical_not(is_end))
                def _():
                    raw_copy(s, 1, nlev - 1 - lev).start()

    lax.fori_loop(steps // 2, steps, prepare, 0)
    den_copies = []
    for r, peer in enumerate(peers):
        copy = remote(
            dens.at[lev], dens.at[lev],
            d_send.at[r], d_recv.at[r], (me, peer),
        )
        copy.start()
        den_copies.append(copy)

    def mix_levels(s):
        @pl.when(jnp.logical_not(is_end))
        def _():
            raw_copy(s, 0, mate).wait_recv()
            raw_copy(s, 1, mate).wait_recv()
            raw_copy(s, 2, mate).wait_recv()
            for i in range(lon_here):
                for z in range(nlev):
                    pad[0:lev_here] = levs[s, z, i]
                    high, low = split(pad[...])
                    rhs[z * KPAD:(z + 1) * KPAD] = high
                    rhs[(nlev + z) * KPAD:(nlev + z + 1) * KPAD] = low
                both = jnp.dot(mix[...], rhs[...], preferred_element_type=jnp.float32)
                first = both[0:PAD] + both[PAD:2 * PAD]
                second = both[2 * PAD:3 * PAD] + both[3 * PAD:4 * PAD]
                gathered[s, 0, i] = jnp.where(parity == 0, first, second)[0:lev_here]
                mixed[s, i] = jnp.where(parity == 0, second, first)[0:lev_here]
            mixed_copy(s).start()

        @pl.when(is_end)
        def _():
            mixed_copy(s).wait_recv()

    orders = [bits[::-1], bits[-2:0:-1] + bits[-1:] + bits[:1]]

    def masks_at(s, p):
        held = [0]
        for bit in orders[s % 2][:p]:
            held = held + [m + bit for m in held]
        return held

    def block_copy(s, m, bit):
        return remote(
            gathered.at[s, m], gathered.at[s, m + bit],
            g_send.at[s, m + bit], g_recv.at[s, m + bit], (flip(me, bit), lev),
        )

    def forward(s, p):
        order = orders[s % 2]
        fresh = [0] if p == 0 else [m + order[p - 1] for m in masks_at(s, p - 1)]
        for m in fresh:
            if p > 0:
                block_copy(s, m - order[p - 1], order[p - 1]).wait_recv()
            for bit in order[p:]:
                copy = block_copy(s, m, bit)
                copy.start()
                pending.append(copy)

    rows = GROUP * lon_here * PAD
    hops = len(bits)

    def load_columns(s):
        for m in range(tiles):
            group, inner = m // GROUP, m % GROUP
            for i in range(lon_here):
                pad[0:lev_here] = gathered[s, m, i]
                value = pad[0:PAD] if i == 0 else jnp.concatenate([value, pad[0:PAD]], axis=0)
            high, low = split(value)
            at = inner * lon_here * PAD
            lhs[group, at:at + lon_here * PAD] = high
            lhs[group, rows + at:rows + at + lon_here * PAD] = low

    num_copies = {}

    def sample(s, part):
        def one_step(nb, carry):
            at = pl.ds(pl.multiple_of(nb * NB, NB), NB)
            hot = onehot[:, at]
            lon_ids = jnp.broadcast_to(lon_of[:, at], (PAD, NB))

            def one_group(group, acc):
                found = jnp.dot(lhs[group], hot, preferred_element_type=jnp.float32)
                for inner in range(GROUP):
                    tile = jnp.bitwise_xor(me, group * GROUP + inner)
                    for i in range(lon_here):
                        r = (inner * lon_here + i) * PAD
                        block = found[r:r + PAD] + found[rows + r:rows + r + PAD]
                        acc = jnp.where(lon_ids == tile * lon_here + i, block, acc)
                return acc

            acc = jnp.zeros((PAD, NB), jnp.float32)
            if tiles == GROUP:
                acc = one_group(0, acc)
            else:
                acc = lax.fori_loop(0, tiles // GROUP, one_group, acc)
            terms = acc[0:lev_here] * weight[:, at]
            nums[s, lev, :, at] = jnp.sum(terms, axis=0, keepdims=True)
            return carry

        lax.fori_loop(part * steps // 2, (part + 1) * steps // 2, one_step, 0)
        at = pl.ds(part * (snd // 2), snd // 2)
        num_copies[(s, part)] = []
        for r, peer in enumerate(peers):
            copy = remote(
                nums.at[s, lev, :, at], nums.at[s, lev, :, at],
                n_send.at[s, part, r], n_recv.at[s, part, r], (me, peer),
            )
            copy.start()
            num_copies[(s, part)].append(copy)

    mix_levels(0)
    forward(0, 0)
    out[0] = gathered[0, 0]
    forward(0, 1)
    mix_levels(1)
    forward(1, 0)
    out[1] = gathered[1, 0]
    for p in range(2, hops + 1):
        forward(0, p)
        if p < hops:
            forward(1, p - 1)
    load_columns(0)
    sample(0, 0)
    forward(1, hops - 1)
    sample(0, 1)
    forward(1, hops)
    load_columns(1)
    sample(1, 0)
    sample(1, 1)

    for copy in den_copies:
        copy.wait_recv()
    den = dens[0]
    for z in range(1, nlev):
        den = den + dens[z]
    in_use = lax.broadcasted_iota(jnp.int32, (1, snd), 1) < counts[0]
    for s in range(scen):
        for part in range(2):
            for copy in num_copies[(s, part)]:
                copy.wait_recv()
            pending.extend(num_copies[(s, part)])
        num = nums[s, 0]
        for z in range(1, nlev):
            num = num + nums[s, z]
        evolved[s] = jnp.where(in_use, num / den, 0.0)
    pending.extend(den_copies)
    for copy in pending:
        copy.wait_send()
    for s in range(scen):
        @pl.when(is_end)
        def _():
            raw_copy(s, 2, nlev - 1 - mate).wait_send()
            raw_copy(s, 0, mate).wait_send()

        @pl.when(jnp.logical_not(is_end))
        def _():
            raw_copy(s, 1, nlev - 1 - lev).wait_send()
            mixed_copy(s).wait_send()


def body(
    tracer, u_courant, v_courant, surface_flux, mixing, kernel, column, owner_tile, offset, counts
):
    scen, lev_here, lon_here, nlat = tracer.shape
    snd = column.shape[0]
    tiles, nlev = lax.axis_size("tile"), lax.axis_size("lev")
    lev = lax.axis_index("lev")
    first = lev // 2 * 2 * lev_here
    rows = lax.dynamic_slice_in_dim(mixing, first, 2 * lev_here, 0)
    rows = rows.reshape(2, lev_here, nlev, lev_here)
    rows = jnp.pad(rows, ((0, 0), (0, PAD - lev_here), (0, 0), (0, KPAD - lev_here)))
    rows = rows.reshape(2, 1, PAD, nlev * KPAD)
    high = lax.reduce_precision(rows, 8, 7)
    low = rows - high
    mix = jnp.concatenate(
        [
            jnp.concatenate([high, high], axis=3),
            jnp.concatenate([low, jnp.zeros_like(low)], axis=3),
        ],
        axis=1,
    )
    mix = mix.reshape(4 * PAD, 2 * nlev * KPAD).astype(jnp.bfloat16)
    f32, bf16 = jnp.float32, jnp.bfloat16
    block = (lev_here, nlat)
    dma = pltpu.SemaphoreType.DMA
    vmem = pl.BlockSpec(memory_space=pltpu.VMEM)
    groups = tiles // GROUP
    out, evolved = pl.pallas_call(
        functools.partial(kernel_body, (scen, lev_here, lon_here, nlat, snd, tiles, nlev)),
        out_shape=(
            jax.ShapeDtypeStruct((scen, lon_here) + block, f32),
            jax.ShapeDtypeStruct((scen, 1, snd), f32),
        ),
        in_specs=[vmem] * 9 + [pl.BlockSpec(memory_space=pltpu.SMEM)],
        out_specs=(vmem, vmem),
        scratch_shapes=[
            pltpu.VMEM((NSUB, scen, lon_here) + block, f32),
            pltpu.VMEM((NSUB, scen) + block, f32),
            pltpu.VMEM((NSUB, scen) + block, f32),
            pltpu.VMEM(block, f32),
            pltpu.VMEM((scen, nlev, lon_here) + block, f32),
            pltpu.VMEM((scen, lon_here) + block, f32),
            pltpu.VMEM((2 * nlev * KPAD, nlat), bf16),
            pltpu.VMEM((scen, tiles, lon_here) + block, f32),
            pltpu.VMEM((groups, 2 * GROUP * lon_here * PAD, nlat), bf16),
            pltpu.VMEM((nlat, snd), bf16),
            pltpu.VMEM((1, snd), jnp.int32),
            pltpu.VMEM((lev_here, snd), f32),
            pltpu.VMEM((scen, nlev, 1, snd), f32),
            pltpu.VMEM((nlev, 1, snd), f32),
            pltpu.VMEM((KPAD, nlat), f32),
            dma((NSUB, scen, 2)),
            dma((NSUB, scen, 2)),
            dma((2,)),
            dma((scen, 4)),
            dma((scen, 4)),
            dma((scen, tiles)),
            dma((scen, tiles)),
            dma((scen, 2, nlev - 1)),
            dma((scen, 2, nlev - 1)),
            dma((nlev - 1,)),
            dma((nlev - 1,)),
        ],
        compiler_params=pltpu.CompilerParams(
            collective_id=0, has_side_effects=True, vmem_limit_bytes=56 * 2**20
        ),
    )(
        tracer.transpose(0, 2, 1, 3),
        u_courant.transpose(1, 0, 2),
        v_courant.transpose(1, 0, 2),
        surface_flux,
        mix,
        kernel,
        column[None],
        owner_tile[None],
        offset[None],
        counts,
    )
    return out.transpose(0, 2, 1, 3), evolved[:, 0]


def solution(mesh):
    in_specs = (
        P(None, "lev", "tile", None),
        P("lev", "tile", None),
        P("lev", "tile", None),
        P(None, "tile", None),
        P(),
        P("lev", "tile"),
        P("tile"),
        P("tile"),
        P("tile"),
        P("tile"),
    )
    out_specs = (P(None, "lev", "tile", None), P(None, "tile"))
    return jax.shard_map(body, mesh=mesh, in_specs=in_specs, out_specs=out_specs, check_vma=False)
```

```python
import functools
import jax
import jax.numpy as jnp
from jax import lax
from jax.experimental import pallas as pl
from jax.experimental.pallas import tpu as pltpu
from jax.sharding import PartitionSpec as P

NSUB = 2
PAD = 24
KPAD = 32
NB = 256
CHUNKS = 4
GROUP = 8
MESH = pl.DeviceIdType.MESH


def split(x):
    high = x.astype(jnp.bfloat16)
    low = (x - high.astype(jnp.float32)).astype(jnp.bfloat16)
    return high, low


def grow(x, rows):
    return jnp.concatenate([x, jnp.zeros((rows - x.shape[0], x.shape[1]), x.dtype)], axis=0)


def flip(index, bit):
    return index + bit - 2 * bit * ((index // bit) % 2)


def substep(cells, winds, lat_winds, lat_ids):
    count = len(lat_winds)
    size = cells[0].shape[-1]
    west = [
        winds[i] * jnp.where(winds[i] > 0, cells[i], cells[i + 1]) for i in range(count + 1)
    ]
    result = []
    for i in range(count):
        centre = cells[i + 1]
        south_cells = pltpu.roll(centre, 1, 1)
        south = lat_winds[i] * jnp.where(lat_winds[i] > 0, south_cells, centre)
        south = jnp.where(lat_ids > 0, south, 0.0)
        north = pltpu.roll(south, size - 1, 1)
        result.append(centre - (west[i + 1] - west[i]) - (north - south))
    return result


def kernel_body(
    dims,
    tracer, u_ref, v_ref, flux, mix, kern, column, owner, offset, counts,
    out, evolved,
    cur, halo_w, halo_e, halo_u, mixed, mixed_in, rhs, gathered, levs, lhs, onehot, lon_of,
    weight, eff, eff_out, nums, dens,
    h_send, h_recv, u_sem, z_send, z_recv, w_send, w_recv, g_send, g_recv, n_send, n_recv,
    d_send, d_recv,
):
    scen, lev_here, lon_here, nlat, snd, tiles, nlev = dims
    me, lev = lax.axis_index("tile"), lax.axis_index("lev")
    east, west = lax.rem(me + 1, tiles), lax.rem(me + tiles - 1, tiles)
    bits = [1 << k for k in range(tiles.bit_length() - 1)]
    peers = [lax.rem(lev + r, nlev) for r in range(1, nlev)]

    barrier = pltpu.get_barrier_semaphore()
    friends = [(east, lev), (west, lev)]
    friends += [(flip(me, b), lev) for b in bits]
    friends += [(me, p) for p in peers]
    for friend in friends:
        pl.semaphore_signal(barrier, inc=1, device_id=friend, device_id_type=MESH)

    row_ids = lax.broadcasted_iota(jnp.int32, (lev_here, nlat), 0)
    lat_ids = lax.broadcasted_iota(jnp.int32, (lev_here, nlat), 1)
    bottom = jnp.logical_and(row_ids == 0, lev == 0)
    for s in range(scen):
        for i in range(lon_here):
            here = tracer[s, i]
            cur[0, s, i] = jnp.where(bottom, here + flux[s, pl.ds(i, 1)], here)
    pl.semaphore_wait(barrier, len(friends))

    def remote(src, dst, send, recv, device):
        return pltpu.make_async_remote_copy(
            src_ref=src, dst_ref=dst, send_sem=send, recv_sem=recv,
            device_id=device, device_id_type=MESH,
        )

    pending = []

    def send_halo(step, s):
        to_east = remote(
            cur.at[step, s, lon_here - 1], halo_w.at[step, s],
            h_send.at[step, s, 0], h_recv.at[step, s, 0], (east, lev),
        )
        to_west = remote(
            cur.at[step, s, 0], halo_e.at[step, s],
            h_send.at[step, s, 1], h_recv.at[step, s, 1], (west, lev),
        )
        to_east.start()
        to_west.start()
        pending.extend([to_east, to_west])
        return to_east, to_west

    u_copy = remote(u_ref.at[0], halo_u, u_sem.at[0], u_sem.at[1], (west, lev))
    u_copy.start()
    pending.append(u_copy)
    halos = {(0, s): send_halo(0, s) for s in range(scen)}

    steps = snd // NB
    half, parity = lev // 2, lev % 2
    is_end = half == parity
    is_inner = jnp.logical_not(is_end)
    mate = half * 2 + 1 - parity
    level_ids = lev * lev_here + lax.broadcasted_iota(jnp.int32, (lev_here, NB), 0)
    width = snd // CHUNKS

    def weigh(nb, carry):
        at = pl.ds(pl.multiple_of(nb * NB, NB), NB)
        used_weight = jnp.where(level_ids >= offset[:, at], kern[:, at], 0.0)
        weight[lev, :, at] = used_weight
        dens[lev, :, at] = jnp.sum(used_weight, axis=0, keepdims=True)
        return carry

    lax.fori_loop(0, steps, weigh, 0)

    def weight_copy(c, k, to):
        part = weight.at[lev, :, pl.ds(c * width, width)]
        return remote(part, part, w_send.at[c, k], w_recv.at[c, k], (me, to))

    def eff_copy(c):
        at = pl.ds(c * width, width)
        return remote(
            eff_out.at[:, at], eff.at[:, at], w_send.at[c, 3], w_recv.at[c, 3], (me, mate)
        )

    def raw_copy(s, k, to):
        return remote(
            levs.at[s, lev], levs.at[s, lev], z_send.at[s, k], z_recv.at[s, k], (me, to)
        )

    def mixed_copy(s):
        return remote(
            mixed.at[s], mixed_in.at[s], z_send.at[s, 3], z_recv.at[s, 3], (me, mate)
        )

    @pl.when(is_end)
    def _():
        for c in range(CHUNKS):
            weight_copy(c, 2, nlev - 1 - mate).start()
            weight_copy(c, 0, mate).start()

    @pl.when(is_inner)
    def _():
        for c in range(CHUNKS):
            weight_copy(c, 1, nlev - 1 - lev).start()

    den_copies = []
    for r, peer in enumerate(peers):
        copy = remote(
            dens.at[lev], dens.at[lev],
            d_send.at[r], d_recv.at[r], (me, peer),
        )
        copy.start()
        den_copies.append(copy)

    lat_rows = lax.broadcasted_iota(jnp.int32, (nlat, NB), 0)

    def prepare(nb, carry):
        at = pl.ds(pl.multiple_of(nb * NB, NB), NB)
        col = column[:, at]
        lon_in = col // nlat
        lat = col - lon_in * nlat
        onehot[:, at] = (lat_rows == lat).astype(jnp.float32).astype(jnp.bfloat16)
        lon_of[:, at] = owner[:, at] * lon_here + lon_in
        return carry

    def mix_blocks(kind, blocks):
        for z, block in enumerate(blocks):
            high, low = split(grow(block, KPAD))
            rhs[z * KPAD:(z + 1) * KPAD] = high
            rhs[(nlev + z) * KPAD:(nlev + z + 1) * KPAD] = low
        both = jnp.dot(mix[kind], rhs[...], preferred_element_type=jnp.float32)
        first = both[0:PAD] + both[PAD:2 * PAD]
        second = both[2 * PAD:3 * PAD] + both[3 * PAD:4 * PAD]
        own = jnp.where(parity == 0, first, second)
        other = jnp.where(parity == 0, second, first)
        return own[0:lev_here], other[0:lev_here]

    def mix_weights(c):
        @pl.when(is_inner)
        def _():
            for k in range(3):
                weight_copy(c, k, mate).wait_recv()
            for n in range(c * width, (c + 1) * width, nlat):
                at = pl.ds(n, nlat)
                own, other = mix_blocks(1, [weight[z, :, at] for z in range(nlev)])
                eff[:, at] = own
                eff_out[:, at] = other
            eff_copy(c).start()

    def wait_weights(c):
        @pl.when(is_end)
        def _():
            eff_copy(c).wait_recv()

    def mix_levels(s):
        @pl.when(is_inner)
        def _():
            for k in range(3):
                raw_copy(s, k, mate).wait_recv()
            for i in range(lon_here):
                own, other = mix_blocks(0, [levs[s, z, i] for z in range(nlev)])
                out[s, i] = own
                mixed[s, i] = other
            mixed_copy(s).start()

    orders = [bits[::-1], bits[-2:0:-1] + bits[-1:] + bits[:1]]

    def masks_at(s, p):
        held = [0]
        for bit in orders[s % 2][:p]:
            held = held + [m + bit for m in held]
        return held

    def block_copy(s, m, bit):
        return remote(
            gathered.at[s, m], gathered.at[s, m + bit],
            g_send.at[s, m + bit], g_recv.at[s, m + bit], (flip(me, bit), lev),
        )

    def forward(s, p):
        order = orders[s % 2]
        fresh = [0] if p == 0 else [m + order[p - 1] for m in masks_at(s, p - 1)]
        for m in fresh:
            if p > 0:
                block_copy(s, m - order[p - 1], order[p - 1]).wait_recv()
            for bit in order[p:]:
                copy = block_copy(s, m, bit)
                copy.start()
                pending.append(copy)

        for m in fresh:
            load_columns(s, m)

    rows = GROUP * lon_here * PAD
    hops = len(bits)

    def load_columns(s, m):
        blocks = [grow(gathered[s, m, i], PAD) for i in range(lon_here)]
        high, low = split(jnp.concatenate(blocks, axis=0))
        at = m % GROUP * lon_here * PAD
        lhs[s, m // GROUP, at:at + lon_here * PAD, 0:nlat] = high
        lhs[s, m // GROUP, at:at + lon_here * PAD, nlat:2 * nlat] = low

    num_copies = {}

    def sample(s, part):
        def one_step(nb, carry):
            at = pl.ds(pl.multiple_of(nb * NB, NB), NB)
            hot = onehot[:, at]
            twice = jnp.concatenate([hot, hot], axis=0)
            lon_ids = jnp.broadcast_to(lon_of[:, at], (PAD, NB))

            def one_group(group, acc):
                found = jnp.dot(lhs[s, group], twice, preferred_element_type=jnp.float32)
                for inner in range(GROUP):
                    tile = jnp.bitwise_xor(me, group * GROUP + inner)
                    for i in range(lon_here):
                        r = (inner * lon_here + i) * PAD
                        block = found[r:r + PAD]
                        acc = jnp.where(lon_ids == tile * lon_here + i, block, acc)
                return acc

            acc = jnp.zeros((PAD, NB), jnp.float32)
            if tiles == GROUP:
                acc = one_group(0, acc)
            else:
                acc = lax.fori_loop(0, tiles // GROUP, one_group, acc)
            terms = acc[0:lev_here] * eff[:, at]
            nums[s, lev, :, at] = jnp.sum(terms, axis=0, keepdims=True)
            return carry

        lax.fori_loop(part * steps // 2, (part + 1) * steps // 2, one_step, 0)
        at = pl.ds(part * (snd // 2), snd // 2)
        num_copies[(s, part)] = []
        for r, peer in enumerate(peers):
            copy = remote(
                nums.at[s, lev, :, at], nums.at[s, lev, :, at],
                n_send.at[s, part, r], n_recv.at[s, part, r], (me, peer),
            )
            copy.start()
            num_copies[(s, part)].append(copy)

    lax.fori_loop(0, steps // 2, prepare, 0)
    u_copy.wait_recv()
    for step in range(NSUB):
        for s in range(scen):
            for copy in halos[(step, s)]:
                copy.wait_recv()
            cells = [halo_w[step, s]] + [cur[step, s, i] for i in range(lon_here)]
            cells.append(halo_e[step, s])
            winds = [u_ref[i] for i in range(lon_here)] + [halo_u[...]]
            new = substep(cells, winds, [v_ref[i] for i in range(lon_here)], lat_ids)
            if step < NSUB - 1:
                for i in range(lon_here):
                    cur[step + 1, s, i] = new[i]
                halos[(step + 1, s)] = send_halo(step + 1, s)
                continue
            for i in range(lon_here):
                gathered[s, 0, i] = new[i]
                levs[s, lev, i] = new[i]

            forward(s, 0)

            @pl.when(is_end)
            def _():
                raw_copy(s, 2, nlev - 1 - mate).start()
                raw_copy(s, 0, mate).start()

            @pl.when(is_inner)
            def _():
                raw_copy(s, 1, nlev - 1 - lev).start()
        if step == 0:
            lax.fori_loop(steps // 2, steps, prepare, 0)

    mix_weights(0)
    forward(0, 1)
    forward(1, 1)
    mix_weights(1)
    for p in range(2, hops):
        forward(0, p)
        if p < hops - 1:
            forward(1, p)
    mix_weights(2)
    forward(0, hops)
    forward(1, hops - 1)
    mix_weights(3)
    wait_weights(0)
    wait_weights(1)
    sample(0, 0)
    forward(1, hops)
    wait_weights(2)
    wait_weights(3)
    sample(0, 1)
    sample(1, 0)
    mix_levels(0)
    sample(1, 1)
    mix_levels(1)

    for copy in den_copies:
        copy.wait_recv()
    den = dens[0]
    for z in range(1, nlev):
        den = den + dens[z]
    in_use = lax.broadcasted_iota(jnp.int32, (1, snd), 1) < counts[0]
    for s in range(scen):
        for part in range(2):
            for copy in num_copies[(s, part)]:
                copy.wait_recv()
            pending.extend(num_copies[(s, part)])
        num = nums[s, 0]
        for z in range(1, nlev):
            num = num + nums[s, z]
        evolved[s] = jnp.where(in_use, num / den, 0.0)
    pending.extend(den_copies)
    for copy in pending:
        copy.wait_send()
    for s in range(scen):
        @pl.when(is_end)
        def _():
            mixed_copy(s).wait_recv()
            out[s] = mixed_in[s]
            raw_copy(s, 2, nlev - 1 - mate).wait_send()
            raw_copy(s, 0, mate).wait_send()

        @pl.when(is_inner)
        def _():
            raw_copy(s, 1, nlev - 1 - lev).wait_send()
            mixed_copy(s).wait_send()
    for c in range(CHUNKS):
        @pl.when(is_end)
        def _():
            weight_copy(c, 2, nlev - 1 - mate).wait_send()
            weight_copy(c, 0, mate).wait_send()

        @pl.when(is_inner)
        def _():
            weight_copy(c, 1, nlev - 1 - lev).wait_send()
            eff_copy(c).wait_send()


def body(
    tracer, u_courant, v_courant, surface_flux, mixing, kernel, column, owner_tile, offset, counts
):
    scen, lev_here, lon_here, nlat = tracer.shape
    snd = column.shape[0]
    tiles, nlev = lax.axis_size("tile"), lax.axis_size("lev")
    lev = lax.axis_index("lev")
    first = lev // 2 * 2 * lev_here
    rows = lax.dynamic_slice_in_dim(
        jnp.stack([mixing, mixing.T]), first, 2 * lev_here, 1
    )
    rows = rows.reshape(2, 2, lev_here, nlev, lev_here)
    rows = jnp.pad(rows, ((0, 0), (0, 0), (0, PAD - lev_here), (0, 0), (0, KPAD - lev_here)))
    rows = rows.reshape(2, 2, 1, PAD, nlev * KPAD)
    high = lax.reduce_precision(rows, 8, 7)
    low = rows - high
    mix = jnp.concatenate(
        [
            jnp.concatenate([high, high], axis=4),
            jnp.concatenate([low, jnp.zeros_like(low)], axis=4),
        ],
        axis=2,
    )
    mix = mix.reshape(2, 4 * PAD, 2 * nlev * KPAD).astype(jnp.bfloat16)
    f32, bf16 = jnp.float32, jnp.bfloat16
    block = (lev_here, nlat)
    dma = pltpu.SemaphoreType.DMA
    vmem = pl.BlockSpec(memory_space=pltpu.VMEM)
    groups = tiles // GROUP
    out, evolved = pl.pallas_call(
        functools.partial(kernel_body, (scen, lev_here, lon_here, nlat, snd, tiles, nlev)),
        out_shape=(
            jax.ShapeDtypeStruct((scen, lon_here) + block, f32),
            jax.ShapeDtypeStruct((scen, 1, snd), f32),
        ),
        in_specs=[vmem] * 9 + [pl.BlockSpec(memory_space=pltpu.SMEM)],
        out_specs=(vmem, vmem),
        scratch_shapes=[
            pltpu.VMEM((NSUB, scen, lon_here) + block, f32),
            pltpu.VMEM((NSUB, scen) + block, f32),
            pltpu.VMEM((NSUB, scen) + block, f32),
            pltpu.VMEM(block, f32),
            pltpu.VMEM((scen, lon_here) + block, f32),
            pltpu.VMEM((scen, lon_here) + block, f32),
            pltpu.VMEM((2 * nlev * KPAD, nlat), bf16),
            pltpu.VMEM((scen, tiles, lon_here) + block, f32),
            pltpu.VMEM((scen, nlev, lon_here) + block, f32),
            pltpu.VMEM((scen, groups, GROUP * lon_here * PAD, 2 * nlat), bf16),
            pltpu.VMEM((nlat, snd), bf16),
            pltpu.VMEM((1, snd), jnp.int32),
            pltpu.VMEM((nlev, lev_here, snd), f32),
            pltpu.VMEM((lev_here, snd), f32),
            pltpu.VMEM((lev_here, snd), f32),
            pltpu.VMEM((scen, nlev, 1, snd), f32),
            pltpu.VMEM((nlev, 1, snd), f32),
            dma((NSUB, scen, 2)),
            dma((NSUB, scen, 2)),
            dma((2,)),
            dma((scen, 4)),
            dma((scen, 4)),
            dma((CHUNKS, 4)),
            dma((CHUNKS, 4)),
            dma((scen, tiles)),
            dma((scen, tiles)),
            dma((scen, 2, nlev - 1)),
            dma((scen, 2, nlev - 1)),
            dma((nlev - 1,)),
            dma((nlev - 1,)),
        ],
        compiler_params=pltpu.CompilerParams(
            collective_id=0, has_side_effects=True, vmem_limit_bytes=56 * 2**20
        ),
    )(
        tracer.transpose(0, 2, 1, 3),
        u_courant.transpose(1, 0, 2),
        v_courant.transpose(1, 0, 2),
        surface_flux,
        mix,
        kernel,
        column[None],
        owner_tile[None],
        offset[None],
        counts,
    )
    return out.transpose(0, 2, 1, 3), evolved[:, 0]


def solution(mesh):
    in_specs = (
        P(None, "lev", "tile", None),
        P("lev", "tile", None),
        P("lev", "tile", None),
        P(None, "tile", None),
        P(),
        P("lev", "tile"),
        P("tile"),
        P("tile"),
        P("tile"),
        P("tile"),
    )
    out_specs = (P(None, "lev", "tile", None), P(None, "tile"))
    return jax.shard_map(body, mesh=mesh, in_specs=in_specs, out_specs=out_specs, check_vma=False)
```

```python
import functools
import jax
import jax.numpy as jnp
from jax import lax
from jax.experimental import pallas as pl
from jax.experimental.pallas import tpu as pltpu
from jax.sharding import PartitionSpec as P

NSUB = 2
PAD = 24
KPAD = 32
NB = 256
CHUNKS = 4
GROUP = 4
MESH = pl.DeviceIdType.MESH


def split(x):
    high = x.astype(jnp.bfloat16)
    low = (x - high.astype(jnp.float32)).astype(jnp.bfloat16)
    return high, low


def grow(x, rows):
    return jnp.concatenate([x, jnp.zeros((rows - x.shape[0], x.shape[1]), x.dtype)], axis=0)


def flip(index, bit):
    return index + bit - 2 * bit * ((index // bit) % 2)


def substep(cells, winds, lat_winds, lat_ids):
    count = len(lat_winds)
    size = cells[0].shape[-1]
    west = [
        winds[i] * jnp.where(winds[i] > 0, cells[i], cells[i + 1]) for i in range(count + 1)
    ]
    result = []
    for i in range(count):
        centre = cells[i + 1]
        south_cells = pltpu.roll(centre, 1, 1)
        south = lat_winds[i] * jnp.where(lat_winds[i] > 0, south_cells, centre)
        south = jnp.where(lat_ids > 0, south, 0.0)
        north = pltpu.roll(south, size - 1, 1)
        result.append(centre - (west[i + 1] - west[i]) - (north - south))
    return result


def kernel_body(
    dims,
    tracer, u_ref, v_ref, flux, mix, kern, column, owner, offset, counts,
    out, evolved,
    cur, halo_w, halo_e, halo_u, mixed, mixed_in, rhs, gathered, levs, lhs, onehot, lon_of,
    weight, eff, eff_out, found_at, nums, dens,
    h_send, h_recv, u_sem, z_send, z_recv, w_send, w_recv, g_send, g_recv, n_send, n_recv,
    d_send, d_recv,
):
    scen, lev_here, lon_here, nlat, snd, tiles, nlev = dims
    me, lev = lax.axis_index("tile"), lax.axis_index("lev")
    east, west = lax.rem(me + 1, tiles), lax.rem(me + tiles - 1, tiles)
    bits = [1 << k for k in range(tiles.bit_length() - 1)]
    peers = [lax.rem(lev + r, nlev) for r in range(1, nlev)]

    barrier = pltpu.get_barrier_semaphore()
    friends = [(east, lev), (west, lev)]
    friends += [(flip(me, b), lev) for b in bits]
    friends += [(me, p) for p in peers]
    for friend in friends:
        pl.semaphore_signal(barrier, inc=1, device_id=friend, device_id_type=MESH)

    row_ids = lax.broadcasted_iota(jnp.int32, (lev_here, nlat), 0)
    lat_ids = lax.broadcasted_iota(jnp.int32, (lev_here, nlat), 1)
    bottom = jnp.logical_and(row_ids == 0, lev == 0)
    for s in range(scen):
        for i in range(lon_here):
            here = tracer[s, i]
            cur[0, s, i] = jnp.where(bottom, here + flux[s, pl.ds(i, 1)], here)
    pl.semaphore_wait(barrier, len(friends))

    def remote(src, dst, send, recv, device):
        return pltpu.make_async_remote_copy(
            src_ref=src, dst_ref=dst, send_sem=send, recv_sem=recv,
            device_id=device, device_id_type=MESH,
        )

    pending = []

    def send_halo(step, s):
        to_east = remote(
            cur.at[step, s, lon_here - 1], halo_w.at[step, s],
            h_send.at[step, s, 0], h_recv.at[step, s, 0], (east, lev),
        )
        to_west = remote(
            cur.at[step, s, 0], halo_e.at[step, s],
            h_send.at[step, s, 1], h_recv.at[step, s, 1], (west, lev),
        )
        to_east.start()
        to_west.start()
        pending.extend([to_east, to_west])
        return to_east, to_west

    u_copy = remote(u_ref.at[0], halo_u, u_sem.at[0], u_sem.at[1], (west, lev))
    u_copy.start()
    pending.append(u_copy)
    halos = {(0, s): send_halo(0, s) for s in range(scen)}

    steps = snd // NB
    half, parity = lev // 2, lev % 2
    is_end = half == parity
    is_inner = jnp.logical_not(is_end)
    mate = half * 2 + 1 - parity
    level_ids = lev * lev_here + lax.broadcasted_iota(jnp.int32, (lev_here, NB), 0)
    width = snd // CHUNKS

    def weigh(nb, carry):
        at = pl.ds(pl.multiple_of(nb * NB, NB), NB)
        used_weight = jnp.where(level_ids >= offset[:, at], kern[:, at], 0.0)
        weight[lev, :, at] = used_weight
        dens[lev, :, at] = jnp.sum(used_weight, axis=0, keepdims=True)
        return carry

    lax.fori_loop(0, steps, weigh, 0)

    def weight_copy(c, k, to):
        part = weight.at[lev, :, pl.ds(c * width, width)]
        return remote(part, part, w_send.at[c, k], w_recv.at[c, k], (me, to))

    def eff_copy(c):
        at = pl.ds(c * width, width)
        return remote(
            eff_out.at[:, at], eff.at[:, at], w_send.at[c, 3], w_recv.at[c, 3], (me, mate)
        )

    def raw_copy(s, k, to):
        return remote(
            levs.at[s, lev], levs.at[s, lev], z_send.at[s, k], z_recv.at[s, k], (me, to)
        )

    def mixed_copy(s):
        return remote(
            mixed.at[s], mixed_in.at[s], z_send.at[s, 3], z_recv.at[s, 3], (me, mate)
        )

    @pl.when(is_end)
    def _():
        for c in range(CHUNKS):
            weight_copy(c, 2, nlev - 1 - mate).start()
            weight_copy(c, 0, mate).start()

    @pl.when(is_inner)
    def _():
        for c in range(CHUNKS):
            weight_copy(c, 1, nlev - 1 - lev).start()

    den_copies = []
    for r, peer in enumerate(peers):
        copy = remote(
            dens.at[lev], dens.at[lev],
            d_send.at[r], d_recv.at[r], (me, peer),
        )
        copy.start()
        den_copies.append(copy)

    lat_rows = lax.broadcasted_iota(jnp.int32, (nlat, NB), 0)

    def prepare(nb, carry):
        at = pl.ds(pl.multiple_of(nb * NB, NB), NB)
        col = column[:, at]
        lon_in = col // nlat
        lat = col - lon_in * nlat
        onehot[:, at] = (lat_rows == lat).astype(jnp.float32).astype(jnp.bfloat16)
        lon_of[:, at] = owner[:, at] * lon_here + lon_in
        return carry

    def mix_blocks(kind, blocks):
        for z, block in enumerate(blocks):
            high, low = split(grow(block, KPAD))
            rhs[z * KPAD:(z + 1) * KPAD] = high
            rhs[(nlev + z) * KPAD:(nlev + z + 1) * KPAD] = low
        both = jnp.dot(mix[kind], rhs[...], preferred_element_type=jnp.float32)
        first = both[0:PAD] + both[PAD:2 * PAD]
        second = both[2 * PAD:3 * PAD] + both[3 * PAD:4 * PAD]
        own = jnp.where(parity == 0, first, second)
        other = jnp.where(parity == 0, second, first)
        return own[0:lev_here], other[0:lev_here]

    def mix_weights(c):
        @pl.when(is_inner)
        def _():
            for k in range(3):
                weight_copy(c, k, mate).wait_recv()
            for n in range(c * width, (c + 1) * width, nlat):
                at = pl.ds(n, nlat)
                own, other = mix_blocks(1, [weight[z, :, at] for z in range(nlev)])
                eff[:, at] = own
                eff_out[:, at] = other
            eff_copy(c).start()

    def wait_weights(c):
        @pl.when(is_end)
        def _():
            eff_copy(c).wait_recv()

    def mix_levels(s):
        @pl.when(is_inner)
        def _():
            for k in range(3):
                raw_copy(s, k, mate).wait_recv()
            for i in range(lon_here):
                own, other = mix_blocks(0, [levs[s, z, i] for z in range(nlev)])
                out[s, i] = own
                mixed[s, i] = other
            mixed_copy(s).start()

    orders = [bits[::-1], bits[-2:0:-1] + bits[-1:] + bits[:1]]

    def masks_at(s, p):
        held = [0]
        for bit in orders[s % 2][:p]:
            held = held + [m + bit for m in held]
        return held

    def block_copy(s, m, bit):
        return remote(
            gathered.at[s, m], gathered.at[s, m + bit],
            g_send.at[s, m + bit], g_recv.at[s, m + bit], (flip(me, bit), lev),
        )

    def forward(s, p):
        order = orders[s % 2]
        fresh = [0] if p == 0 else [m + order[p - 1] for m in masks_at(s, p - 1)]
        for m in fresh:
            if p > 0:
                block_copy(s, m - order[p - 1], order[p - 1]).wait_recv()
            for bit in order[p:]:
                copy = block_copy(s, m, bit)
                copy.start()
                pending.append(copy)

        for m in fresh:
            load_columns(s, m)

    hops = len(bits) - 1

    def arrivals(s):
        return [m + c for m in masks_at(s, hops) for c in range(2)]

    def load_columns(s, m):
        blocks = [grow(gathered[s, m, i], PAD) for i in range(lon_here)]
        high, low = split(jnp.concatenate(blocks, axis=0))
        place = arrivals(s).index(m)
        at = place % GROUP * lon_here * PAD
        lhs[s, place // GROUP, at:at + lon_here * PAD, 0:nlat] = high
        lhs[s, place // GROUP, at:at + lon_here * PAD, nlat:2 * nlat] = low

    groups = tiles // GROUP

    num_copies = {}

    def search(s, group, low, high):
        slots = arrivals(s)[group * GROUP:(group + 1) * GROUP]
        for m in slots:
            if m % 2 == 1:
                block_copy(s, m - 1, 1).wait_recv()
                load_columns(s, m)
        resume(s, group, low, high)

    def resume(s, group, low, high):
        slots = arrivals(s)[group * GROUP:(group + 1) * GROUP]

        def one_step(nb, carry):
            at = pl.ds(pl.multiple_of(nb * NB, NB), NB)
            hot = onehot[:, at]
            twice = jnp.concatenate([hot, hot], axis=0)
            lon_ids = jnp.broadcast_to(lon_of[:, at], (PAD, NB))
            found = jnp.dot(lhs[s, group], twice, preferred_element_type=jnp.float32)
            acc = jnp.zeros((PAD, NB), jnp.float32) if group == 0 else found_at[s, :, at]
            for inner, m in enumerate(slots):
                tile = jnp.bitwise_xor(me, m)
                for i in range(lon_here):
                    r = (inner * lon_here + i) * PAD
                    acc = jnp.where(lon_ids == tile * lon_here + i, found[r:r + PAD], acc)
            if group < groups - 1:
                found_at[s, :, at] = acc
            else:
                terms = acc[0:lev_here] * eff[:, at]
                nums[s, lev, :, at] = jnp.sum(terms, axis=0, keepdims=True)
            return carry

        lax.fori_loop(low, high, one_step, 0, unroll=2)

    def send_nums(s, part):
        at = pl.ds(part * (snd // 2), snd // 2)
        num_copies[(s, part)] = []
        for r, peer in enumerate(peers):
            copy = remote(
                nums.at[s, lev, :, at], nums.at[s, lev, :, at],
                n_send.at[s, part, r], n_recv.at[s, part, r], (me, peer),
            )
            copy.start()
            num_copies[(s, part)].append(copy)

    lax.fori_loop(0, steps // 2, prepare, 0)
    u_copy.wait_recv()
    for step in range(NSUB):
        for s in range(scen):
            for copy in halos[(step, s)]:
                copy.wait_recv()
            cells = [halo_w[step, s]] + [cur[step, s, i] for i in range(lon_here)]
            cells.append(halo_e[step, s])
            winds = [u_ref[i] for i in range(lon_here)] + [halo_u[...]]
            new = substep(cells, winds, [v_ref[i] for i in range(lon_here)], lat_ids)
            if step < NSUB - 1:
                for i in range(lon_here):
                    cur[step + 1, s, i] = new[i]
                halos[(step + 1, s)] = send_halo(step + 1, s)
                continue
            for i in range(lon_here):
                gathered[s, 0, i] = new[i]
                levs[s, lev, i] = new[i]

            forward(s, 0)

            @pl.when(is_end)
            def _():
                raw_copy(s, 2, nlev - 1 - mate).start()
                raw_copy(s, 0, mate).start()

            @pl.when(is_inner)
            def _():
                raw_copy(s, 1, nlev - 1 - lev).start()
        if step == 0:
            lax.fori_loop(steps // 2, steps, prepare, 0)

    mix_weights(0)
    forward(0, 1)
    forward(1, 1)
    search(0, 0, 0, steps)
    forward(0, 2)
    mix_weights(1)
    search(1, 0, 0, steps)
    forward(1, 2)
    for p in range(3, hops + 1):
        forward(0, p)
        forward(1, p)
    mix_weights(2)
    for group in range(1, groups - 1):
        search(0, group, 0, steps)
        search(1, group, 0, steps)
    mix_weights(3)
    wait_weights(0)
    wait_weights(1)
    search(0, groups - 1, 0, steps // 2)
    send_nums(0, 0)
    wait_weights(2)
    wait_weights(3)
    resume(0, groups - 1, steps // 2, steps)
    send_nums(0, 1)
    mix_levels(0)
    search(1, groups - 1, 0, steps // 2)
    send_nums(1, 0)
    mix_levels(1)
    resume(1, groups - 1, steps // 2, steps)
    send_nums(1, 1)

    for copy in den_copies:
        copy.wait_recv()
    den = dens[0]
    for z in range(1, nlev):
        den = den + dens[z]
    in_use = lax.broadcasted_iota(jnp.int32, (1, snd), 1) < counts[0]
    for s in range(scen):
        for part in range(2):
            for copy in num_copies[(s, part)]:
                copy.wait_recv()
            pending.extend(num_copies[(s, part)])
        num = nums[s, 0]
        for z in range(1, nlev):
            num = num + nums[s, z]
        evolved[s] = jnp.where(in_use, num / den, 0.0)
    pending.extend(den_copies)
    for copy in pending:
        copy.wait_send()
    for s in range(scen):
        @pl.when(is_end)
        def _():
            mixed_copy(s).wait_recv()
            out[s] = mixed_in[s]
            raw_copy(s, 2, nlev - 1 - mate).wait_send()
            raw_copy(s, 0, mate).wait_send()

        @pl.when(is_inner)
        def _():
            raw_copy(s, 1, nlev - 1 - lev).wait_send()
            mixed_copy(s).wait_send()
    for c in range(CHUNKS):
        @pl.when(is_end)
        def _():
            weight_copy(c, 2, nlev - 1 - mate).wait_send()
            weight_copy(c, 0, mate).wait_send()

        @pl.when(is_inner)
        def _():
            weight_copy(c, 1, nlev - 1 - lev).wait_send()
            eff_copy(c).wait_send()


def body(
    tracer, u_courant, v_courant, surface_flux, mixing, kernel, column, owner_tile, offset, counts
):
    scen, lev_here, lon_here, nlat = tracer.shape
    snd = column.shape[0]
    tiles, nlev = lax.axis_size("tile"), lax.axis_size("lev")
    lev = lax.axis_index("lev")
    first = lev // 2 * 2 * lev_here
    rows = lax.dynamic_slice_in_dim(
        jnp.stack([mixing, mixing.T]), first, 2 * lev_here, 1
    )
    rows = rows.reshape(2, 2, lev_here, nlev, lev_here)
    rows = jnp.pad(rows, ((0, 0), (0, 0), (0, PAD - lev_here), (0, 0), (0, KPAD - lev_here)))
    rows = rows.reshape(2, 2, 1, PAD, nlev * KPAD)
    high = lax.reduce_precision(rows, 8, 7)
    low = rows - high
    mix = jnp.concatenate(
        [
            jnp.concatenate([high, high], axis=4),
            jnp.concatenate([low, jnp.zeros_like(low)], axis=4),
        ],
        axis=2,
    )
    mix = mix.reshape(2, 4 * PAD, 2 * nlev * KPAD).astype(jnp.bfloat16)
    f32, bf16 = jnp.float32, jnp.bfloat16
    block = (lev_here, nlat)
    dma = pltpu.SemaphoreType.DMA
    vmem = pl.BlockSpec(memory_space=pltpu.VMEM)
    groups = tiles // GROUP
    out, evolved = pl.pallas_call(
        functools.partial(kernel_body, (scen, lev_here, lon_here, nlat, snd, tiles, nlev)),
        out_shape=(
            jax.ShapeDtypeStruct((scen, lon_here) + block, f32),
            jax.ShapeDtypeStruct((scen, 1, snd), f32),
        ),
        in_specs=[vmem] * 9 + [pl.BlockSpec(memory_space=pltpu.SMEM)],
        out_specs=(vmem, vmem),
        scratch_shapes=[
            pltpu.VMEM((NSUB, scen, lon_here) + block, f32),
            pltpu.VMEM((NSUB, scen) + block, f32),
            pltpu.VMEM((NSUB, scen) + block, f32),
            pltpu.VMEM(block, f32),
            pltpu.VMEM((scen, lon_here) + block, f32),
            pltpu.VMEM((scen, lon_here) + block, f32),
            pltpu.VMEM((2 * nlev * KPAD, nlat), bf16),
            pltpu.VMEM((scen, tiles, lon_here) + block, f32),
            pltpu.VMEM((scen, nlev, lon_here) + block, f32),
            pltpu.VMEM((scen, groups, GROUP * lon_here * PAD, 2 * nlat), bf16),
            pltpu.VMEM((nlat, snd), bf16),
            pltpu.VMEM((1, snd), jnp.int32),
            pltpu.VMEM((nlev, lev_here, snd), f32),
            pltpu.VMEM((lev_here, snd), f32),
            pltpu.VMEM((lev_here, snd), f32),
            pltpu.VMEM((scen, PAD, snd), f32),
            pltpu.VMEM((scen, nlev, 1, snd), f32),
            pltpu.VMEM((nlev, 1, snd), f32),
            dma((NSUB, scen, 2)),
            dma((NSUB, scen, 2)),
            dma((2,)),
            dma((scen, 4)),
            dma((scen, 4)),
            dma((CHUNKS, 4)),
            dma((CHUNKS, 4)),
            dma((scen, tiles)),
            dma((scen, tiles)),
            dma((scen, 2, nlev - 1)),
            dma((scen, 2, nlev - 1)),
            dma((nlev - 1,)),
            dma((nlev - 1,)),
        ],
        compiler_params=pltpu.CompilerParams(
            collective_id=0, has_side_effects=True, vmem_limit_bytes=56 * 2**20
        ),
    )(
        tracer.transpose(0, 2, 1, 3),
        u_courant.transpose(1, 0, 2),
        v_courant.transpose(1, 0, 2),
        surface_flux,
        mix,
        kernel,
        column[None],
        owner_tile[None],
        offset[None],
        counts,
    )
    return out.transpose(0, 2, 1, 3), evolved[:, 0]


def solution(mesh):
    in_specs = (
        P(None, "lev", "tile", None),
        P("lev", "tile", None),
        P("lev", "tile", None),
        P(None, "tile", None),
        P(),
        P("lev", "tile"),
        P("tile"),
        P("tile"),
        P("tile"),
        P("tile"),
    )
    out_specs = (P(None, "lev", "tile", None), P(None, "tile"))
    return jax.shard_map(body, mesh=mesh, in_specs=in_specs, out_specs=out_specs, check_vma=False)
```

```python
import functools
import jax
import jax.numpy as jnp
from jax import lax
from jax.experimental import pallas as pl
from jax.experimental.pallas import tpu as pltpu
from jax.sharding import PartitionSpec as P

NSUB = 2
PAD = 24
KPAD = 32
NB = 256
CHUNKS = 4
GROUP = 4
MESH = pl.DeviceIdType.MESH


def split(x):
    high = x.astype(jnp.bfloat16)
    low = (x - high.astype(jnp.float32)).astype(jnp.bfloat16)
    return high, low


def grow(x, rows):
    return jnp.concatenate([x, jnp.zeros((rows - x.shape[0], x.shape[1]), x.dtype)], axis=0)


def flip(index, bit):
    return index + bit - 2 * bit * ((index // bit) % 2)


def substep(cells, winds, lat_winds, lat_ids):
    count = len(lat_winds)
    size = cells[0].shape[-1]
    west = [
        winds[i] * jnp.where(winds[i] > 0, cells[i], cells[i + 1]) for i in range(count + 1)
    ]
    result = []
    for i in range(count):
        centre = cells[i + 1]
        south_cells = pltpu.roll(centre, 1, 1)
        south = lat_winds[i] * jnp.where(lat_winds[i] > 0, south_cells, centre)
        south = jnp.where(lat_ids > 0, south, 0.0)
        north = pltpu.roll(south, size - 1, 1)
        result.append(centre - (west[i + 1] - west[i]) - (north - south))
    return result


def kernel_body(
    dims,
    tracer, u_in, v_in, flux, mixing, kern, column, owner, offset, counts,
    out, evolved,
    mix, u_ref, cur, halo_w, halo_e, halo_u, mixed, mixed_in, rhs, gathered, levs, lhs, onehot, lon_of,
    weight, eff, eff_out, found_at, nums, dens,
    h_send, h_recv, u_sem, z_send, z_recv, w_send, w_recv, g_send, g_recv, n_send, n_recv,
    d_send, d_recv,
):
    scen, lev_here, lon_here, nlat, snd, tiles, nlev = dims
    me, lev = lax.axis_index("tile"), lax.axis_index("lev")
    east, west = lax.rem(me + 1, tiles), lax.rem(me + tiles - 1, tiles)
    bits = [1 << k for k in range(tiles.bit_length() - 1)]
    peers = [lax.rem(lev + r, nlev) for r in range(1, nlev)]

    barrier = pltpu.get_barrier_semaphore()
    friends = [(east, lev), (west, lev)]
    friends += [(flip(me, b), lev) for b in bits]
    friends += [(me, p) for p in peers]
    for friend in friends:
        pl.semaphore_signal(barrier, inc=1, device_id=friend, device_id_type=MESH)

    row_ids = lax.broadcasted_iota(jnp.int32, (lev_here, nlat), 0)
    lat_ids = lax.broadcasted_iota(jnp.int32, (lev_here, nlat), 1)
    bottom = jnp.logical_and(row_ids == 0, lev == 0)
    for s in range(scen):
        for i in range(lon_here):
            here = tracer[s, :, i, :]
            cur[0, s, i] = jnp.where(bottom, here + flux[s, pl.ds(i, 1), :], here)
    for i in range(lon_here):
        u_ref[i] = u_in[:, i, :]
    pl.semaphore_wait(barrier, len(friends))

    def remote(src, dst, send, recv, device):
        return pltpu.make_async_remote_copy(
            src_ref=src, dst_ref=dst, send_sem=send, recv_sem=recv,
            device_id=device, device_id_type=MESH,
        )

    pending = []

    def send_halo(step, s):
        to_east = remote(
            cur.at[step, s, lon_here - 1], halo_w.at[step, s],
            h_send.at[step, s, 0], h_recv.at[step, s, 0], (east, lev),
        )
        to_west = remote(
            cur.at[step, s, 0], halo_e.at[step, s],
            h_send.at[step, s, 1], h_recv.at[step, s, 1], (west, lev),
        )
        to_east.start()
        to_west.start()
        pending.extend([to_east, to_west])
        return to_east, to_west

    u_copy = remote(u_ref.at[0], halo_u, u_sem.at[0], u_sem.at[1], (west, lev))
    u_copy.start()
    pending.append(u_copy)
    halos = {(0, s): send_halo(0, s) for s in range(scen)}

    steps = snd // NB
    half, parity = lev // 2, lev % 2
    is_end = half == parity
    is_inner = jnp.logical_not(is_end)
    mate = half * 2 + 1 - parity
    level_ids = lev * lev_here + lax.broadcasted_iota(jnp.int32, (lev_here, NB), 0)
    width = snd // CHUNKS

    def weigh(nb, carry):
        at = pl.ds(pl.multiple_of(nb * NB, NB), NB)
        used_weight = jnp.where(level_ids >= offset[:, at], kern[:, at], 0.0)
        weight[lev, :, at] = used_weight
        dens[lev, :, at] = jnp.sum(used_weight, axis=0, keepdims=True)
        return carry

    lax.fori_loop(0, steps, weigh, 0)

    def weight_copy(c, k, to):
        part = weight.at[lev, :, pl.ds(c * width, width)]
        return remote(part, part, w_send.at[c, k], w_recv.at[c, k], (me, to))

    def eff_copy(c):
        at = pl.ds(c * width, width)
        return remote(
            eff_out.at[:, at], eff.at[:, at], w_send.at[c, 3], w_recv.at[c, 3], (me, mate)
        )

    def raw_copy(s, k, to):
        return remote(
            levs.at[s, lev], levs.at[s, lev], z_send.at[s, k], z_recv.at[s, k], (me, to)
        )

    def mixed_copy(s):
        return remote(
            mixed.at[s], mixed_in.at[s], z_send.at[s, 3], z_recv.at[s, 3], (me, mate)
        )

    @pl.when(is_end)
    def _():
        for c in range(CHUNKS):
            weight_copy(c, 2, nlev - 1 - mate).start()
            weight_copy(c, 0, mate).start()

    @pl.when(is_inner)
    def _():
        for c in range(CHUNKS):
            weight_copy(c, 1, nlev - 1 - lev).start()

    den_copies = []
    for r, peer in enumerate(peers):
        copy = remote(
            dens.at[lev], dens.at[lev],
            d_send.at[r], d_recv.at[r], (me, peer),
        )
        copy.start()
        den_copies.append(copy)

    lat_rows = lax.broadcasted_iota(jnp.int32, (nlat, NB), 0)

    def prepare(nb, carry):
        at = pl.ds(pl.multiple_of(nb * NB, NB), NB)
        col = column[:, at]
        lon_in = col // nlat
        lat = col - lon_in * nlat
        onehot[:, at] = (lat_rows == lat).astype(jnp.float32).astype(jnp.bfloat16)
        lon_of[:, at] = owner[:, at] * lon_here + lon_in
        return carry

    def lay_out_mixing():
        size = nlev * lev_here
        row = lax.broadcasted_iota(jnp.int32, (4 * PAD, size), 0)
        col = lax.broadcasted_iota(jnp.int32, (4 * PAD, size), 1)
        part = sum((row >= PAD * q).astype(jnp.int32) for q in range(1, 4))
        inner = row - PAD * part
        second = (part >= 2).astype(jnp.int32)
        wanted = (half * 2 + second) * lev_here + inner
        hit = jnp.logical_and(col == wanted, inner < lev_here)
        is_low = part - 2 * second
        pick_high = jnp.where(jnp.logical_and(hit, is_low == 0), 1.0, 0.0).astype(jnp.bfloat16)
        pick_low = jnp.where(jnp.logical_and(hit, is_low == 1), 1.0, 0.0).astype(jnp.bfloat16)
        at = lax.broadcasted_iota(jnp.int32, (size, nlev * KPAD), 1)
        here = lax.broadcasted_iota(jnp.int32, (size, nlev * KPAD), 0)
        block = sum((at >= KPAD * z).astype(jnp.int32) for z in range(1, nlev))
        inner = at - KPAD * block
        hit = jnp.logical_and(here == block * lev_here + inner, inner < lev_here)
        spread = jnp.where(hit, 1.0, 0.0).astype(jnp.bfloat16)
        high, low = split(mixing[...])

        def dot(a, b, dim):
            return lax.dot_general(
                a, b, (((1,), (dim,)), ((), ())), preferred_element_type=jnp.float32
            )

        for kind in range(2):
            highs = dot(pick_high, high, kind)
            both = highs + dot(pick_low, low, kind)
            for k, rows in enumerate((both, highs)):
                placed = dot(rows.astype(jnp.bfloat16), spread, 0)
                mix[kind, :, k * nlev * KPAD:(k + 1) * nlev * KPAD] = placed.astype(jnp.bfloat16)

    def mix_blocks(kind, blocks):
        for z, block in enumerate(blocks):
            high, low = split(grow(block, KPAD))
            rhs[z * KPAD:(z + 1) * KPAD] = high
            rhs[(nlev + z) * KPAD:(nlev + z + 1) * KPAD] = low
        both = jnp.dot(mix[kind], rhs[...], preferred_element_type=jnp.float32)
        first = both[0:PAD] + both[PAD:2 * PAD]
        second = both[2 * PAD:3 * PAD] + both[3 * PAD:4 * PAD]
        own = jnp.where(parity == 0, first, second)
        other = jnp.where(parity == 0, second, first)
        return own[0:lev_here], other[0:lev_here]

    def mix_weights(c):
        @pl.when(is_inner)
        def _():
            for k in range(3):
                weight_copy(c, k, mate).wait_recv()
            for n in range(c * width, (c + 1) * width, nlat):
                at = pl.ds(n, nlat)
                own, other = mix_blocks(1, [weight[z, :, at] for z in range(nlev)])
                eff[:, at] = own
                eff_out[:, at] = other
            eff_copy(c).start()

    def wait_weights(c):
        @pl.when(is_end)
        def _():
            eff_copy(c).wait_recv()

    def mix_levels(s):
        @pl.when(is_inner)
        def _():
            for k in range(3):
                raw_copy(s, k, mate).wait_recv()
            for i in range(lon_here):
                own, other = mix_blocks(0, [levs[s, z, i] for z in range(nlev)])
                out[s, :, i, :] = own
                mixed[s, i] = other
            mixed_copy(s).start()

    orders = [bits[::-1], bits[-2:0:-1] + bits[-1:] + bits[:1]]

    def masks_at(s, p):
        held = [0]
        for bit in orders[s % 2][:p]:
            held = held + [m + bit for m in held]
        return held

    def block_copy(s, m, bit):
        return remote(
            gathered.at[s, m], gathered.at[s, m + bit],
            g_send.at[s, m + bit], g_recv.at[s, m + bit], (flip(me, bit), lev),
        )

    def forward(s, p):
        order = orders[s % 2]
        fresh = [0] if p == 0 else [m + order[p - 1] for m in masks_at(s, p - 1)]
        for m in fresh:
            if p > 0:
                block_copy(s, m - order[p - 1], order[p - 1]).wait_recv()
            for bit in order[p:]:
                copy = block_copy(s, m, bit)
                copy.start()
                pending.append(copy)

        for m in fresh:
            load_columns(s, m)

    hops = len(bits) - 1

    def arrivals(s):
        return [m + c for m in masks_at(s, hops) for c in range(2)]

    def load_columns(s, m):
        blocks = [grow(gathered[s, m, i], PAD) for i in range(lon_here)]
        high, low = split(jnp.concatenate(blocks, axis=0))
        place = arrivals(s).index(m)
        at = place % GROUP * lon_here * PAD
        lhs[s, place // GROUP, at:at + lon_here * PAD, 0:nlat] = high
        lhs[s, place // GROUP, at:at + lon_here * PAD, nlat:2 * nlat] = low

    groups = tiles // GROUP

    num_copies = {}

    def search(s, group, low, high):
        slots = arrivals(s)[group * GROUP:(group + 1) * GROUP]
        for m in slots:
            if m % 2 == 1:
                block_copy(s, m - 1, 1).wait_recv()
                load_columns(s, m)
        resume(s, group, low, high)

    def resume(s, group, low, high):
        slots = arrivals(s)[group * GROUP:(group + 1) * GROUP]

        def one_step(nb, carry):
            at = pl.ds(pl.multiple_of(nb * NB, NB), NB)
            hot = onehot[:, at]
            twice = jnp.concatenate([hot, hot], axis=0)
            lon_ids = jnp.broadcast_to(lon_of[:, at], (PAD, NB))
            found = jnp.dot(lhs[s, group], twice, preferred_element_type=jnp.float32)
            acc = jnp.zeros((PAD, NB), jnp.float32) if group == 0 else found_at[s, :, at]
            for inner, m in enumerate(slots):
                tile = jnp.bitwise_xor(me, m)
                for i in range(lon_here):
                    r = (inner * lon_here + i) * PAD
                    acc = jnp.where(lon_ids == tile * lon_here + i, found[r:r + PAD], acc)
            if group < groups - 1:
                found_at[s, :, at] = acc
            else:
                terms = acc[0:lev_here] * eff[:, at]
                nums[s, lev, :, at] = jnp.sum(terms, axis=0, keepdims=True)
            return carry

        lax.fori_loop(low, high, one_step, 0, unroll=2)

    def send_nums(s, part):
        at = pl.ds(part * (snd // 2), snd // 2)
        num_copies[(s, part)] = []
        for r, peer in enumerate(peers):
            copy = remote(
                nums.at[s, lev, :, at], nums.at[s, lev, :, at],
                n_send.at[s, part, r], n_recv.at[s, part, r], (me, peer),
            )
            copy.start()
            num_copies[(s, part)].append(copy)

    lay_out_mixing()
    lax.fori_loop(0, steps // 2, prepare, 0)
    u_copy.wait_recv()
    for step in range(NSUB):
        for s in range(scen):
            for copy in halos[(step, s)]:
                copy.wait_recv()
            cells = [halo_w[step, s]] + [cur[step, s, i] for i in range(lon_here)]
            cells.append(halo_e[step, s])
            winds = [u_ref[i] for i in range(lon_here)] + [halo_u[...]]
            new = substep(cells, winds, [v_in[:, i, :] for i in range(lon_here)], lat_ids)
            if step < NSUB - 1:
                for i in range(lon_here):
                    cur[step + 1, s, i] = new[i]
                halos[(step + 1, s)] = send_halo(step + 1, s)
                continue
            for i in range(lon_here):
                gathered[s, 0, i] = new[i]
                levs[s, lev, i] = new[i]

            forward(s, 0)

            @pl.when(is_end)
            def _():
                raw_copy(s, 2, nlev - 1 - mate).start()
                raw_copy(s, 0, mate).start()

            @pl.when(is_inner)
            def _():
                raw_copy(s, 1, nlev - 1 - lev).start()
        if step == 0:
            lax.fori_loop(steps // 2, steps, prepare, 0)

    mix_weights(0)
    forward(0, 1)
    forward(1, 1)
    search(0, 0, 0, steps)
    forward(0, 2)
    mix_weights(1)
    search(1, 0, 0, steps)
    forward(1, 2)
    for p in range(3, hops + 1):
        forward(0, p)
        forward(1, p)
    mix_weights(2)
    for group in range(1, groups - 1):
        search(0, group, 0, steps)
        search(1, group, 0, steps)
    mix_weights(3)
    wait_weights(0)
    wait_weights(1)
    search(0, groups - 1, 0, steps // 2)
    send_nums(0, 0)
    wait_weights(2)
    wait_weights(3)
    resume(0, groups - 1, steps // 2, steps)
    send_nums(0, 1)
    search(1, groups - 1, 0, steps // 2)
    send_nums(1, 0)
    resume(1, groups - 1, steps // 2, steps)
    send_nums(1, 1)
    mix_levels(0)
    mix_levels(1)

    for copy in den_copies:
        copy.wait_recv()
    den = dens[0]
    for z in range(1, nlev):
        den = den + dens[z]
    in_use = lax.broadcasted_iota(jnp.int32, (1, snd), 1) < counts[0]
    for s in range(scen):
        for part in range(2):
            for copy in num_copies[(s, part)]:
                copy.wait_recv()
            pending.extend(num_copies[(s, part)])
        num = nums[s, 0]
        for z in range(1, nlev):
            num = num + nums[s, z]
        evolved[pl.ds(s, 1), :] = jnp.where(in_use, num / den, 0.0)
    pending.extend(den_copies)
    for copy in pending:
        copy.wait_send()
    for s in range(scen):
        @pl.when(is_end)
        def _():
            mixed_copy(s).wait_recv()
            for i in range(lon_here):
                out[s, :, i, :] = mixed_in[s, i]
            raw_copy(s, 2, nlev - 1 - mate).wait_send()
            raw_copy(s, 0, mate).wait_send()

        @pl.when(is_inner)
        def _():
            raw_copy(s, 1, nlev - 1 - lev).wait_send()
            mixed_copy(s).wait_send()
    for c in range(CHUNKS):
        @pl.when(is_end)
        def _():
            weight_copy(c, 2, nlev - 1 - mate).wait_send()
            weight_copy(c, 0, mate).wait_send()

        @pl.when(is_inner)
        def _():
            weight_copy(c, 1, nlev - 1 - lev).wait_send()
            eff_copy(c).wait_send()


def body(
    tracer, u_courant, v_courant, surface_flux, mixing, kernel, column, owner_tile, offset, counts
):
    scen, lev_here, lon_here, nlat = tracer.shape
    snd = column.shape[0]
    tiles, nlev = lax.axis_size("tile"), lax.axis_size("lev")
    f32, bf16 = jnp.float32, jnp.bfloat16
    block = (lev_here, nlat)
    dma = pltpu.SemaphoreType.DMA
    vmem = pl.BlockSpec(memory_space=pltpu.VMEM)
    groups = tiles // GROUP
    out, evolved = pl.pallas_call(
        functools.partial(kernel_body, (scen, lev_here, lon_here, nlat, snd, tiles, nlev)),
        out_shape=(
            jax.ShapeDtypeStruct(tracer.shape, f32),
            jax.ShapeDtypeStruct((scen, snd), f32),
        ),
        in_specs=[vmem] * 9 + [pl.BlockSpec(memory_space=pltpu.SMEM)],
        out_specs=(vmem, vmem),
        scratch_shapes=[
            pltpu.VMEM((2, 4 * PAD, 2 * nlev * KPAD), bf16),
            pltpu.VMEM((lon_here,) + block, f32),
            pltpu.VMEM((NSUB, scen, lon_here) + block, f32),
            pltpu.VMEM((NSUB, scen) + block, f32),
            pltpu.VMEM((NSUB, scen) + block, f32),
            pltpu.VMEM(block, f32),
            pltpu.VMEM((scen, lon_here) + block, f32),
            pltpu.VMEM((scen, lon_here) + block, f32),
            pltpu.VMEM((2 * nlev * KPAD, nlat), bf16),
            pltpu.VMEM((scen, tiles, lon_here) + block, f32),
            pltpu.VMEM((scen, nlev, lon_here) + block, f32),
            pltpu.VMEM((scen, groups, GROUP * lon_here * PAD, 2 * nlat), bf16),
            pltpu.VMEM((nlat, snd), bf16),
            pltpu.VMEM((1, snd), jnp.int32),
            pltpu.VMEM((nlev, lev_here, snd), f32),
            pltpu.VMEM((lev_here, snd), f32),
            pltpu.VMEM((lev_here, snd), f32),
            pltpu.VMEM((scen, PAD, snd), f32),
            pltpu.VMEM((scen, nlev, 1, snd), f32),
            pltpu.VMEM((nlev, 1, snd), f32),
            dma((NSUB, scen, 2)),
            dma((NSUB, scen, 2)),
            dma((2,)),
            dma((scen, 4)),
            dma((scen, 4)),
            dma((CHUNKS, 4)),
            dma((CHUNKS, 4)),
            dma((scen, tiles)),
            dma((scen, tiles)),
            dma((scen, 2, nlev - 1)),
            dma((scen, 2, nlev - 1)),
            dma((nlev - 1,)),
            dma((nlev - 1,)),
        ],
        compiler_params=pltpu.CompilerParams(
            collective_id=0, has_side_effects=True, vmem_limit_bytes=56 * 2**20
        ),
    )(
        tracer,
        u_courant,
        v_courant,
        surface_flux,
        mixing,
        kernel,
        column[None],
        owner_tile[None],
        offset[None],
        counts,
    )
    return out, evolved


def solution(mesh):
    in_specs = (
        P(None, "lev", "tile", None),
        P("lev", "tile", None),
        P("lev", "tile", None),
        P(None, "tile", None),
        P(),
        P("lev", "tile"),
        P("tile"),
        P("tile"),
        P("tile"),
        P("tile"),
    )
    out_specs = (P(None, "lev", "tile", None), P(None, "tile"))
    return jax.shard_map(body, mesh=mesh, in_specs=in_specs, out_specs=out_specs, check_vma=False)
```

```python
import functools
import jax
import jax.numpy as jnp
from jax import lax
from jax.experimental import pallas as pl
from jax.experimental.pallas import tpu as pltpu
from jax.sharding import PartitionSpec as P

NSUB = 2
PAD = 24
KPAD = 32
NB = 256
CHUNKS = 4
GROUP = 4
MESH = pl.DeviceIdType.MESH


def split(x):
    high = x.astype(jnp.bfloat16)
    low = (x - high.astype(jnp.float32)).astype(jnp.bfloat16)
    return high, low


def grow(x, rows):
    return jnp.concatenate([x, jnp.zeros((rows - x.shape[0], x.shape[1]), x.dtype)], axis=0)


def flip(index, bit):
    return index + bit - 2 * bit * ((index // bit) % 2)


def substep(cells, winds, lat_winds, lat_ids):
    count = len(lat_winds)
    size = cells[0].shape[-1]
    west = [
        winds[i] * jnp.where(winds[i] > 0, cells[i], cells[i + 1]) for i in range(count + 1)
    ]
    result = []
    for i in range(count):
        centre = cells[i + 1]
        south_cells = pltpu.roll(centre, 1, 1)
        south = lat_winds[i] * jnp.where(lat_winds[i] > 0, south_cells, centre)
        south = jnp.where(lat_ids > 0, south, 0.0)
        north = pltpu.roll(south, size - 1, 1)
        result.append(centre - (west[i + 1] - west[i]) - (north - south))
    return result


def kernel_body(
    dims,
    tracer, u_in, v_in, flux, mixing, kern, column, owner, offset, counts,
    out, evolved,
    mix, u_ref, cur, halo_w, halo_e, halo_u, mixed, mixed_in, rhs, gathered, levs, lhs, onehot, lon_of,
    weight, eff, eff_out, found_at, nums, dens,
    h_send, h_recv, u_sem, z_send, z_recv, w_send, w_recv, g_send, g_recv, n_send, n_recv,
    d_send, d_recv,
):
    scen, lev_here, lon_here, nlat, snd, tiles, nlev = dims
    me, lev = lax.axis_index("tile"), lax.axis_index("lev")
    east, west = lax.rem(me + 1, tiles), lax.rem(me + tiles - 1, tiles)
    bits = [1 << k for k in range(tiles.bit_length() - 1)]
    peers = [lax.rem(lev + r, nlev) for r in range(1, nlev)]

    barrier = pltpu.get_barrier_semaphore()
    friends = [(east, lev), (west, lev)]
    friends += [(flip(me, b), lev) for b in bits]
    friends += [(me, p) for p in peers]
    for friend in friends:
        pl.semaphore_signal(barrier, inc=1, device_id=friend, device_id_type=MESH)

    row_ids = lax.broadcasted_iota(jnp.int32, (lev_here, nlat), 0)
    lat_ids = lax.broadcasted_iota(jnp.int32, (lev_here, nlat), 1)
    bottom = jnp.logical_and(row_ids == 0, lev == 0)
    for s in range(scen):
        for i in range(lon_here):
            here = tracer[s, :, i, :]
            cur[0, s, i] = jnp.where(bottom, here + flux[s, pl.ds(i, 1), :], here)
    for i in range(lon_here):
        u_ref[i] = u_in[:, i, :]
    pl.semaphore_wait(barrier, len(friends))

    def remote(src, dst, send, recv, device):
        return pltpu.make_async_remote_copy(
            src_ref=src, dst_ref=dst, send_sem=send, recv_sem=recv,
            device_id=device, device_id_type=MESH,
        )

    pending = []

    def send_halo(step, s):
        to_east = remote(
            cur.at[step, s, lon_here - 1], halo_w.at[step, s],
            h_send.at[step, s, 0], h_recv.at[step, s, 0], (east, lev),
        )
        to_west = remote(
            cur.at[step, s, 0], halo_e.at[step, s],
            h_send.at[step, s, 1], h_recv.at[step, s, 1], (west, lev),
        )
        to_east.start()
        to_west.start()
        pending.extend([to_east, to_west])
        return to_east, to_west

    u_copy = remote(u_ref.at[0], halo_u, u_sem.at[0], u_sem.at[1], (west, lev))
    u_copy.start()
    pending.append(u_copy)
    halos = {(0, s): send_halo(0, s) for s in range(scen)}

    steps = snd // NB
    half, parity = lev // 2, lev % 2
    is_end = half == parity
    is_inner = jnp.logical_not(is_end)
    mate = half * 2 + 1 - parity
    level_ids = lev * lev_here + lax.broadcasted_iota(jnp.int32, (lev_here, NB), 0)
    width = snd // CHUNKS

    def weigh(nb, carry):
        at = pl.ds(pl.multiple_of(nb * NB, NB), NB)
        used_weight = jnp.where(level_ids >= offset[:, at], kern[:, at], 0.0)
        weight[lev, :, at] = used_weight
        dens[lev, :, at] = jnp.sum(used_weight, axis=0, keepdims=True)
        return carry

    lax.fori_loop(0, steps, weigh, 0)

    def weight_copy(c, k, to):
        part = weight.at[lev, :, pl.ds(c * width, width)]
        return remote(part, part, w_send.at[c, k], w_recv.at[c, k], (me, to))

    def eff_copy(c):
        at = pl.ds(c * width, width)
        return remote(
            eff_out.at[:, at], eff.at[:, at], w_send.at[c, 3], w_recv.at[c, 3], (me, mate)
        )

    def raw_copy(s, k, to):
        return remote(
            levs.at[s, lev], levs.at[s, lev], z_send.at[s, k], z_recv.at[s, k], (me, to)
        )

    def mixed_copy(s):
        return remote(
            mixed.at[s], mixed_in.at[s], z_send.at[s, 3], z_recv.at[s, 3], (me, mate)
        )

    @pl.when(is_end)
    def _():
        for c in range(CHUNKS):
            weight_copy(c, 2, nlev - 1 - mate).start()
            weight_copy(c, 0, mate).start()

    @pl.when(is_inner)
    def _():
        for c in range(CHUNKS):
            weight_copy(c, 1, nlev - 1 - lev).start()

    den_copies = []
    for r, peer in enumerate(peers):
        copy = remote(
            dens.at[lev], dens.at[lev],
            d_send.at[r], d_recv.at[r], (me, peer),
        )
        copy.start()
        den_copies.append(copy)

    lat_rows = lax.broadcasted_iota(jnp.int32, (nlat, NB), 0)

    def prepare(nb, carry):
        at = pl.ds(pl.multiple_of(nb * NB, NB), NB)
        col = column[:, at]
        lon_in = col // nlat
        lat = col - lon_in * nlat
        onehot[:, at] = (lat_rows == lat).astype(jnp.float32).astype(jnp.bfloat16)
        lon_of[:, at] = owner[:, at] * lon_here + lon_in
        return carry

    def lay_out_mixing():
        size = nlev * lev_here
        row = lax.broadcasted_iota(jnp.int32, (4 * PAD, size), 0)
        col = lax.broadcasted_iota(jnp.int32, (4 * PAD, size), 1)
        part = sum((row >= PAD * q).astype(jnp.int32) for q in range(1, 4))
        inner = row - PAD * part
        second = (part >= 2).astype(jnp.int32)
        wanted = (half * 2 + second) * lev_here + inner
        hit = jnp.logical_and(col == wanted, inner < lev_here)
        is_low = part - 2 * second
        pick_high = jnp.where(jnp.logical_and(hit, is_low == 0), 1.0, 0.0).astype(jnp.bfloat16)
        pick_low = jnp.where(jnp.logical_and(hit, is_low == 1), 1.0, 0.0).astype(jnp.bfloat16)
        at = lax.broadcasted_iota(jnp.int32, (size, nlev * KPAD), 1)
        here = lax.broadcasted_iota(jnp.int32, (size, nlev * KPAD), 0)
        block = sum((at >= KPAD * z).astype(jnp.int32) for z in range(1, nlev))
        inner = at - KPAD * block
        hit = jnp.logical_and(here == block * lev_here + inner, inner < lev_here)
        spread = jnp.where(hit, 1.0, 0.0).astype(jnp.bfloat16)
        high, low = split(mixing[...])

        def dot(a, b, dim):
            return lax.dot_general(
                a, b, (((1,), (dim,)), ((), ())), preferred_element_type=jnp.float32
            )

        for kind in range(2):
            highs = dot(pick_high, high, kind)
            both = highs + dot(pick_low, low, kind)
            for k, rows in enumerate((both, highs)):
                placed = dot(rows.astype(jnp.bfloat16), spread, 0)
                mix[kind, :, k * nlev * KPAD:(k + 1) * nlev * KPAD] = placed.astype(jnp.bfloat16)

    def mix_blocks(kind, blocks):
        for z, block in enumerate(blocks):
            high, low = split(grow(block, KPAD))
            rhs[z * KPAD:(z + 1) * KPAD] = high
            rhs[(nlev + z) * KPAD:(nlev + z + 1) * KPAD] = low
        both = jnp.dot(mix[kind], rhs[...], preferred_element_type=jnp.float32)
        first = both[0:PAD] + both[PAD:2 * PAD]
        second = both[2 * PAD:3 * PAD] + both[3 * PAD:4 * PAD]
        own = jnp.where(parity == 0, first, second)
        other = jnp.where(parity == 0, second, first)
        return own[0:lev_here], other[0:lev_here]

    def mix_weights(c):
        @pl.when(is_inner)
        def _():
            for k in range(3):
                weight_copy(c, k, mate).wait_recv()
            for n in range(c * width, (c + 1) * width, nlat):
                at = pl.ds(n, nlat)
                own, other = mix_blocks(1, [weight[z, :, at] for z in range(nlev)])
                eff[:, at] = own
                eff_out[:, at] = other
            eff_copy(c).start()

    def wait_weights(c):
        @pl.when(is_end)
        def _():
            eff_copy(c).wait_recv()

    def mix_levels(s):
        @pl.when(is_inner)
        def _():
            for k in range(3):
                raw_copy(s, k, mate).wait_recv()
            for i in range(lon_here):
                own, other = mix_blocks(0, [levs[s, z, i] for z in range(nlev)])
                out[s, :, i, :] = own
                mixed[s, i] = other
            mixed_copy(s).start()

    orders = [bits[::-1], bits[-2:0:-1] + bits[-1:] + bits[:1]]

    def masks_at(s, p):
        held = [0]
        for bit in orders[s % 2][:p]:
            held = held + [m + bit for m in held]
        return held

    def block_copy(s, m, bit):
        return remote(
            gathered.at[s, m], gathered.at[s, m + bit],
            g_send.at[s, m + bit], g_recv.at[s, m + bit], (flip(me, bit), lev),
        )

    def forward(s, p):
        order = orders[s % 2]
        fresh = [0] if p == 0 else [m + order[p - 1] for m in masks_at(s, p - 1)]
        for m in fresh:
            if p > 0:
                block_copy(s, m - order[p - 1], order[p - 1]).wait_recv()
            for bit in order[p:]:
                copy = block_copy(s, m, bit)
                copy.start()
                pending.append(copy)

        for m in fresh:
            load_columns(s, m)

    hops = len(bits) - 1

    def arrivals(s):
        return [m + c for m in masks_at(s, hops) for c in range(2)]

    def load_columns(s, m):
        blocks = [grow(gathered[s, m, i], PAD) for i in range(lon_here)]
        high, low = split(jnp.concatenate(blocks, axis=0))
        place = arrivals(s).index(m)
        at = (s * GROUP + place % GROUP) * lon_here * PAD
        lhs[place // GROUP, at:at + lon_here * PAD, 0:nlat] = high
        lhs[place // GROUP, at:at + lon_here * PAD, nlat:2 * nlat] = low

    groups = tiles // GROUP

    num_copies = {}

    def complete(group):
        for s in range(scen):
            for m in arrivals(s)[group * GROUP:(group + 1) * GROUP]:
                if m % 2 == 1:
                    block_copy(s, m - 1, 1).wait_recv()
                    load_columns(s, m)

    def search(group, part):
        pieces = range(0, PAD, 8)

        def one_step(nb, carry):
            at = pl.ds(pl.multiple_of(nb * NB, NB), NB)
            hot = onehot[:, at]
            twice = jnp.concatenate([hot, hot], axis=0)
            lon_ids = jnp.broadcast_to(lon_of[:, at], (8, NB))
            found = jnp.dot(lhs[group], twice, preferred_element_type=jnp.float32)
            for s in range(scen):
                if group == 0:
                    acc = [jnp.zeros((8, NB), jnp.float32) for _ in pieces]
                else:
                    acc = [found_at[s, q:q + 8, at] for q in pieces]
                slots = arrivals(s)[group * GROUP:(group + 1) * GROUP]
                for inner, m in enumerate(slots):
                    tile = jnp.bitwise_xor(me, m)
                    for i in range(lon_here):
                        r = ((s * GROUP + inner) * lon_here + i) * PAD
                        here = lon_ids == tile * lon_here + i
                        acc = [
                            jnp.where(here, found[r + q:r + q + 8], old)
                            for q, old in zip(pieces, acc)
                        ]
                if group < groups - 1:
                    for q, value in zip(pieces, acc):
                        found_at[s, q:q + 8, at] = value
                else:
                    whole = jnp.concatenate(acc, axis=0)
                    terms = whole[0:lev_here] * eff[:, at]
                    nums[s, lev, :, at] = jnp.sum(terms, axis=0, keepdims=True)
            return carry

        lax.fori_loop(part * steps // 2, (part + 1) * steps // 2, one_step, 0, unroll=2)

    def send_nums(s, part):
        at = pl.ds(part * (snd // 2), snd // 2)
        num_copies[(s, part)] = []
        for r, peer in enumerate(peers):
            copy = remote(
                nums.at[s, lev, :, at], nums.at[s, lev, :, at],
                n_send.at[s, part, r], n_recv.at[s, part, r], (me, peer),
            )
            copy.start()
            num_copies[(s, part)].append(copy)

    lay_out_mixing()
    lax.fori_loop(0, steps // 2, prepare, 0)
    u_copy.wait_recv()
    for step in range(NSUB):
        for s in range(scen):
            for copy in halos[(step, s)]:
                copy.wait_recv()
            cells = [halo_w[step, s]] + [cur[step, s, i] for i in range(lon_here)]
            cells.append(halo_e[step, s])
            winds = [u_ref[i] for i in range(lon_here)] + [halo_u[...]]
            new = substep(cells, winds, [v_in[:, i, :] for i in range(lon_here)], lat_ids)
            if step < NSUB - 1:
                for i in range(lon_here):
                    cur[step + 1, s, i] = new[i]
                halos[(step + 1, s)] = send_halo(step + 1, s)
                continue
            for i in range(lon_here):
                gathered[s, 0, i] = new[i]
                levs[s, lev, i] = new[i]

            forward(s, 0)

            @pl.when(is_end)
            def _():
                raw_copy(s, 2, nlev - 1 - mate).start()
                raw_copy(s, 0, mate).start()

            @pl.when(is_inner)
            def _():
                raw_copy(s, 1, nlev - 1 - lev).start()
        if step == 0:
            lax.fori_loop(steps // 2, steps, prepare, 0)

    mix_weights(0)
    forward(0, 1)
    forward(1, 1)
    complete(0)
    search(0, 0)
    forward(0, 2)
    forward(1, 2)
    mix_weights(1)
    search(0, 1)
    for p in range(3, hops + 1):
        forward(0, p)
        forward(1, p)
    mix_weights(2)
    for group in range(1, groups - 1):
        complete(group)
        search(group, 0)
        search(group, 1)
    mix_weights(3)
    complete(groups - 1)
    wait_weights(0)
    wait_weights(1)
    search(groups - 1, 0)
    send_nums(0, 0)
    send_nums(1, 0)
    wait_weights(2)
    wait_weights(3)
    search(groups - 1, 1)
    send_nums(0, 1)
    send_nums(1, 1)
    mix_levels(0)
    mix_levels(1)

    for copy in den_copies:
        copy.wait_recv()
    den = dens[0]
    for z in range(1, nlev):
        den = den + dens[z]
    in_use = lax.broadcasted_iota(jnp.int32, (1, snd), 1) < counts[0]
    for s in range(scen):
        for part in range(2):
            for copy in num_copies[(s, part)]:
                copy.wait_recv()
            pending.extend(num_copies[(s, part)])
        num = nums[s, 0]
        for z in range(1, nlev):
            num = num + nums[s, z]
        evolved[pl.ds(s, 1), :] = jnp.where(in_use, num / den, 0.0)
    pending.extend(den_copies)
    for copy in pending:
        copy.wait_send()
    for s in range(scen):
        @pl.when(is_end)
        def _():
            mixed_copy(s).wait_recv()
            for i in range(lon_here):
                out[s, :, i, :] = mixed_in[s, i]
            raw_copy(s, 2, nlev - 1 - mate).wait_send()
            raw_copy(s, 0, mate).wait_send()

        @pl.when(is_inner)
        def _():
            raw_copy(s, 1, nlev - 1 - lev).wait_send()
            mixed_copy(s).wait_send()
    for c in range(CHUNKS):
        @pl.when(is_end)
        def _():
            weight_copy(c, 2, nlev - 1 - mate).wait_send()
            weight_copy(c, 0, mate).wait_send()

        @pl.when(is_inner)
        def _():
            weight_copy(c, 1, nlev - 1 - lev).wait_send()
            eff_copy(c).wait_send()


def body(
    tracer, u_courant, v_courant, surface_flux, mixing, kernel, column, owner_tile, offset, counts
):
    scen, lev_here, lon_here, nlat = tracer.shape
    snd = column.shape[0]
    tiles, nlev = lax.axis_size("tile"), lax.axis_size("lev")
    f32, bf16 = jnp.float32, jnp.bfloat16
    block = (lev_here, nlat)
    dma = pltpu.SemaphoreType.DMA
    vmem = pl.BlockSpec(memory_space=pltpu.VMEM)
    groups = tiles // GROUP
    out, evolved = pl.pallas_call(
        functools.partial(kernel_body, (scen, lev_here, lon_here, nlat, snd, tiles, nlev)),
        out_shape=(
            jax.ShapeDtypeStruct(tracer.shape, f32),
            jax.ShapeDtypeStruct((scen, snd), f32),
        ),
        in_specs=[vmem] * 9 + [pl.BlockSpec(memory_space=pltpu.SMEM)],
        out_specs=(vmem, vmem),
        scratch_shapes=[
            pltpu.VMEM((2, 4 * PAD, 2 * nlev * KPAD), bf16),
            pltpu.VMEM((lon_here,) + block, f32),
            pltpu.VMEM((NSUB, scen, lon_here) + block, f32),
            pltpu.VMEM((NSUB, scen) + block, f32),
            pltpu.VMEM((NSUB, scen) + block, f32),
            pltpu.VMEM(block, f32),
            pltpu.VMEM((scen, lon_here) + block, f32),
            pltpu.VMEM((scen, lon_here) + block, f32),
            pltpu.VMEM((2 * nlev * KPAD, nlat), bf16),
            pltpu.VMEM((scen, tiles, lon_here) + block, f32),
            pltpu.VMEM((scen, nlev, lon_here) + block, f32),
            pltpu.VMEM((groups, scen * GROUP * lon_here * PAD, 2 * nlat), bf16),
            pltpu.VMEM((nlat, snd), bf16),
            pltpu.VMEM((1, snd), jnp.int32),
            pltpu.VMEM((nlev, lev_here, snd), f32),
            pltpu.VMEM((lev_here, snd), f32),
            pltpu.VMEM((lev_here, snd), f32),
            pltpu.VMEM((scen, PAD, snd), f32),
            pltpu.VMEM((scen, nlev, 1, snd), f32),
            pltpu.VMEM((nlev, 1, snd), f32),
            dma((NSUB, scen, 2)),
            dma((NSUB, scen, 2)),
            dma((2,)),
            dma((scen, 4)),
            dma((scen, 4)),
            dma((CHUNKS, 4)),
            dma((CHUNKS, 4)),
            dma((scen, tiles)),
            dma((scen, tiles)),
            dma((scen, 2, nlev - 1)),
            dma((scen, 2, nlev - 1)),
            dma((nlev - 1,)),
            dma((nlev - 1,)),
        ],
        compiler_params=pltpu.CompilerParams(
            collective_id=0, has_side_effects=True, vmem_limit_bytes=56 * 2**20
        ),
    )(
        tracer,
        u_courant,
        v_courant,
        surface_flux,
        mixing,
        kernel,
        column[None],
        owner_tile[None],
        offset[None],
        counts,
    )
    return out, evolved


def solution(mesh):
    in_specs = (
        P(None, "lev", "tile", None),
        P("lev", "tile", None),
        P("lev", "tile", None),
        P(None, "tile", None),
        P(),
        P("lev", "tile"),
        P("tile"),
        P("tile"),
        P("tile"),
        P("tile"),
    )
    out_specs = (P(None, "lev", "tile", None), P(None, "tile"))
    return jax.shard_map(body, mesh=mesh, in_specs=in_specs, out_specs=out_specs, check_vma=False)
```

```python
import functools
import jax
import jax.numpy as jnp
from jax import lax
from jax.experimental import pallas as pl
from jax.experimental.pallas import tpu as pltpu
from jax.sharding import PartitionSpec as P

NSUB = 2
PAD = 24
KPAD = 32
NB = 256
CHUNKS = 4
GROUP = 4
MESH = pl.DeviceIdType.MESH


def split(x):
    high = x.astype(jnp.bfloat16)
    low = (x - high.astype(jnp.float32)).astype(jnp.bfloat16)
    return high, low


def grow(x, rows):
    return jnp.concatenate([x, jnp.zeros((rows - x.shape[0], x.shape[1]), x.dtype)], axis=0)


def flip(index, bit):
    return index + bit - 2 * bit * ((index // bit) % 2)


def substep(cells, winds, lat_winds, lat_ids):
    count = len(lat_winds)
    size = cells[0].shape[-1]
    west = [
        winds[i] * jnp.where(winds[i] > 0, cells[i], cells[i + 1]) for i in range(count + 1)
    ]
    result = []
    for i in range(count):
        centre = cells[i + 1]
        south_cells = pltpu.roll(centre, 1, 1)
        south = lat_winds[i] * jnp.where(lat_winds[i] > 0, south_cells, centre)
        south = jnp.where(lat_ids > 0, south, 0.0)
        north = pltpu.roll(south, size - 1, 1)
        result.append(centre - (west[i + 1] - west[i]) - (north - south))
    return result


def kernel_body(
    dims,
    tracer, u_in, v_in, flux, mixing, kern, column, owner, offset, counts,
    out, evolved,
    mix, u_ref, cur, halo_w, halo_e, halo_u, mixed, mixed_in, rhs, gathered, levs, lhs, onehot, lon_of,
    weight, eff, eff_out, found_at, nums, dens,
    h_send, h_recv, u_sem, z_send, z_recv, w_send, w_recv, g_send, g_recv, n_send, n_recv,
    d_send, d_recv,
):
    scen, lev_here, lon_here, nlat, snd, tiles, nlev = dims
    me, lev = lax.axis_index("tile"), lax.axis_index("lev")
    east, west = lax.rem(me + 1, tiles), lax.rem(me + tiles - 1, tiles)
    bits = [1 << k for k in range(tiles.bit_length() - 1)]
    peers = [lax.rem(lev + r, nlev) for r in range(1, nlev)]

    barrier = pltpu.get_barrier_semaphore()
    friends = [(east, lev), (west, lev)]
    friends += [(flip(me, b), lev) for b in bits]
    friends += [(me, p) for p in peers]
    for friend in friends:
        pl.semaphore_signal(barrier, inc=1, device_id=friend, device_id_type=MESH)

    row_ids = lax.broadcasted_iota(jnp.int32, (lev_here, nlat), 0)
    lat_ids = lax.broadcasted_iota(jnp.int32, (lev_here, nlat), 1)
    bottom = jnp.logical_and(row_ids == 0, lev == 0)
    for s in range(scen):
        for i in range(lon_here):
            here = tracer[s, :, i, :]
            cur[0, s, i] = jnp.where(bottom, here + flux[s, pl.ds(i, 1), :], here)
    for i in range(lon_here):
        u_ref[i] = u_in[:, i, :]
    pl.semaphore_wait(barrier, len(friends))

    def remote(src, dst, send, recv, device):
        return pltpu.make_async_remote_copy(
            src_ref=src, dst_ref=dst, send_sem=send, recv_sem=recv,
            device_id=device, device_id_type=MESH,
        )

    pending = []

    def send_halo(step, s):
        to_east = remote(
            cur.at[step, s, lon_here - 1], halo_w.at[step, s],
            h_send.at[step, s, 0], h_recv.at[step, s, 0], (east, lev),
        )
        to_west = remote(
            cur.at[step, s, 0], halo_e.at[step, s],
            h_send.at[step, s, 1], h_recv.at[step, s, 1], (west, lev),
        )
        to_east.start()
        to_west.start()
        pending.extend([to_east, to_west])
        return to_east, to_west

    u_copy = remote(u_ref.at[0], halo_u, u_sem.at[0], u_sem.at[1], (west, lev))
    u_copy.start()
    pending.append(u_copy)
    halos = {(0, s): send_halo(0, s) for s in range(scen)}

    steps = snd // NB
    half, parity = lev // 2, lev % 2
    is_end = half == parity
    is_inner = jnp.logical_not(is_end)
    mate = half * 2 + 1 - parity
    level_ids = lev * lev_here + lax.broadcasted_iota(jnp.int32, (lev_here, NB), 0)
    width = snd // CHUNKS

    def weigh(nb, carry):
        at = pl.ds(pl.multiple_of(nb * NB, NB), NB)
        used_weight = jnp.where(level_ids >= offset[:, at], kern[:, at], 0.0)
        weight[lev, :, at] = used_weight
        dens[lev, :, at] = jnp.sum(used_weight, axis=0, keepdims=True)
        return carry

    lax.fori_loop(0, steps, weigh, 0)

    def weight_copy(c, k, to):
        part = weight.at[lev, :, pl.ds(c * width, width)]
        return remote(part, part, w_send.at[c, k], w_recv.at[c, k], (me, to))

    def eff_copy(c):
        at = pl.ds(c * width, width)
        return remote(
            eff_out.at[:, at], eff.at[:, at], w_send.at[c, 3], w_recv.at[c, 3], (me, mate)
        )

    def raw_copy(s, k, to):
        return remote(
            levs.at[s, lev], levs.at[s, lev], z_send.at[s, k], z_recv.at[s, k], (me, to)
        )

    def mixed_copy(s):
        return remote(
            mixed.at[s], mixed_in.at[s], z_send.at[s, 3], z_recv.at[s, 3], (me, mate)
        )

    @pl.when(is_end)
    def _():
        for c in range(CHUNKS):
            weight_copy(c, 2, nlev - 1 - mate).start()
            weight_copy(c, 0, mate).start()

    @pl.when(is_inner)
    def _():
        for c in range(CHUNKS):
            weight_copy(c, 1, nlev - 1 - lev).start()

    den_copies = []
    for r, peer in enumerate(peers):
        copy = remote(
            dens.at[lev], dens.at[lev],
            d_send.at[r], d_recv.at[r], (me, peer),
        )
        copy.start()
        den_copies.append(copy)

    lat_rows = lax.broadcasted_iota(jnp.int32, (nlat, NB), 0)

    def prepare(nb, carry):
        at = pl.ds(pl.multiple_of(nb * NB, NB), NB)
        col = column[:, at]
        lon_in = col // nlat
        lat = col - lon_in * nlat
        onehot[:, at] = (lat_rows == lat).astype(jnp.float32).astype(jnp.bfloat16)
        lon_of[:, at] = owner[:, at] * lon_here + lon_in
        return carry

    def lay_out_mixing():
        size = nlev * lev_here
        row = lax.broadcasted_iota(jnp.int32, (4 * PAD, size), 0)
        col = lax.broadcasted_iota(jnp.int32, (4 * PAD, size), 1)
        part = sum((row >= PAD * q).astype(jnp.int32) for q in range(1, 4))
        inner = row - PAD * part
        second = (part >= 2).astype(jnp.int32)
        wanted = (half * 2 + second) * lev_here + inner
        hit = jnp.logical_and(col == wanted, inner < lev_here)
        is_low = part - 2 * second
        pick_high = jnp.where(jnp.logical_and(hit, is_low == 0), 1.0, 0.0).astype(jnp.bfloat16)
        pick_low = jnp.where(jnp.logical_and(hit, is_low == 1), 1.0, 0.0).astype(jnp.bfloat16)
        at = lax.broadcasted_iota(jnp.int32, (size, nlev * KPAD), 1)
        here = lax.broadcasted_iota(jnp.int32, (size, nlev * KPAD), 0)
        block = sum((at >= KPAD * z).astype(jnp.int32) for z in range(1, nlev))
        inner = at - KPAD * block
        hit = jnp.logical_and(here == block * lev_here + inner, inner < lev_here)
        spread = jnp.where(hit, 1.0, 0.0).astype(jnp.bfloat16)
        high, low = split(mixing[...])

        def dot(a, b, dim):
            return lax.dot_general(
                a, b, (((1,), (dim,)), ((), ())), preferred_element_type=jnp.float32
            )

        for kind in range(2):
            highs = dot(pick_high, high, kind)
            both = highs + dot(pick_low, low, kind)
            for k, rows in enumerate((both, highs)):
                placed = dot(rows.astype(jnp.bfloat16), spread, 0)
                mix[kind, :, k * nlev * KPAD:(k + 1) * nlev * KPAD] = placed.astype(jnp.bfloat16)

    def mix_blocks(kind, blocks):
        for z, block in enumerate(blocks):
            high, low = split(grow(block, KPAD))
            rhs[z * KPAD:(z + 1) * KPAD] = high
            rhs[(nlev + z) * KPAD:(nlev + z + 1) * KPAD] = low
        both = jnp.dot(mix[kind], rhs[...], preferred_element_type=jnp.float32)
        first = both[0:PAD] + both[PAD:2 * PAD]
        second = both[2 * PAD:3 * PAD] + both[3 * PAD:4 * PAD]
        own = jnp.where(parity == 0, first, second)
        other = jnp.where(parity == 0, second, first)
        return own[0:lev_here], other[0:lev_here]

    def mix_weights(c):
        @pl.when(is_inner)
        def _():
            for k in range(3):
                weight_copy(c, k, mate).wait_recv()
            for n in range(c * width, (c + 1) * width, nlat):
                at = pl.ds(n, nlat)
                own, other = mix_blocks(1, [weight[z, :, at] for z in range(nlev)])
                eff[:, at] = own
                eff_out[:, at] = other
            eff_copy(c).start()

    def wait_weights(c):
        @pl.when(is_end)
        def _():
            eff_copy(c).wait_recv()

    def mix_levels(s):
        @pl.when(is_inner)
        def _():
            for k in range(3):
                raw_copy(s, k, mate).wait_recv()
            for i in range(lon_here):
                own, other = mix_blocks(0, [levs[s, z, i] for z in range(nlev)])
                out[s, :, i, :] = own
                mixed[s, i] = other
            mixed_copy(s).start()

    orders = [bits[::-1], bits[-2:0:-1] + bits[-1:] + bits[:1]]

    def masks_at(s, p):
        held = [0]
        for bit in orders[s % 2][:p]:
            held = held + [m + bit for m in held]
        return held

    def block_copy(s, m, bit):
        return remote(
            gathered.at[s, m], gathered.at[s, m + bit],
            g_send.at[s, m + bit], g_recv.at[s, m + bit], (flip(me, bit), lev),
        )

    def forward(s, p):
        order = orders[s % 2]
        fresh = [0] if p == 0 else [m + order[p - 1] for m in masks_at(s, p - 1)]
        for m in fresh:
            if p > 0:
                block_copy(s, m - order[p - 1], order[p - 1]).wait_recv()
            for bit in order[p:]:
                copy = block_copy(s, m, bit)
                copy.start()
                pending.append(copy)

        for m in fresh:
            load_columns(s, m)

    hops = len(bits) - 1

    def arrivals(s):
        return [m + c for m in masks_at(s, hops) for c in range(2)]

    def load_columns(s, m):
        blocks = [grow(gathered[s, m, i], PAD) for i in range(lon_here)]
        high, low = split(jnp.concatenate(blocks, axis=0))
        place = arrivals(s).index(m)
        at = (s * GROUP + place % GROUP) * lon_here * PAD
        lhs[place // GROUP, at:at + lon_here * PAD, 0:nlat] = high
        lhs[place // GROUP, at:at + lon_here * PAD, nlat:2 * nlat] = low

    groups = tiles // GROUP

    num_copies = {}

    def complete(group):
        for s in range(scen):
            for m in arrivals(s)[group * GROUP:(group + 1) * GROUP]:
                if m % 2 == 1:
                    block_copy(s, m - 1, 1).wait_recv()
                    load_columns(s, m)

    def search(group, part):
        pieces = range(0, PAD, 8)

        def one_step(nb, carry):
            at = pl.ds(pl.multiple_of(nb * NB, NB), NB)
            hot = onehot[:, at]
            twice = jnp.concatenate([hot, hot], axis=0)
            lon_ids = jnp.broadcast_to(lon_of[:, at], (8, NB))
            found = jnp.dot(lhs[group], twice, preferred_element_type=jnp.float32)
            for s in range(scen):
                if group == 0:
                    acc = [jnp.zeros((8, NB), jnp.float32) for _ in pieces]
                else:
                    acc = [found_at[s, q:q + 8, at] for q in pieces]
                slots = arrivals(s)[group * GROUP:(group + 1) * GROUP]
                for inner, m in enumerate(slots):
                    tile = jnp.bitwise_xor(me, m)
                    for i in range(lon_here):
                        r = ((s * GROUP + inner) * lon_here + i) * PAD
                        here = lon_ids == tile * lon_here + i
                        acc = [
                            jnp.where(here, found[r + q:r + q + 8], old)
                            for q, old in zip(pieces, acc)
                        ]
                if group < groups - 1:
                    for q, value in zip(pieces, acc):
                        found_at[s, q:q + 8, at] = value
                else:
                    whole = jnp.concatenate(acc, axis=0)
                    terms = whole[0:lev_here] * eff[:, at]
                    nums[s, lev, :, at] = jnp.sum(terms, axis=0, keepdims=True)
            return carry

        lax.fori_loop(part * steps // 2, (part + 1) * steps // 2, one_step, 0, unroll=2)

    def send_nums(s, part):
        at = pl.ds(part * (snd // 2), snd // 2)
        num_copies[(s, part)] = []
        for r, peer in enumerate(peers):
            copy = remote(
                nums.at[s, lev, :, at], nums.at[s, lev, :, at],
                n_send.at[s, part, r], n_recv.at[s, part, r], (me, peer),
            )
            copy.start()
            num_copies[(s, part)].append(copy)

    lay_out_mixing()
    lax.fori_loop(0, steps // 2, prepare, 0)
    u_copy.wait_recv()
    for step in range(NSUB):
        for s in range(scen):
            for copy in halos[(step, s)]:
                copy.wait_recv()
            cells = [halo_w[step, s]] + [cur[step, s, i] for i in range(lon_here)]
            cells.append(halo_e[step, s])
            winds = [u_ref[i] for i in range(lon_here)] + [halo_u[...]]
            new = substep(cells, winds, [v_in[:, i, :] for i in range(lon_here)], lat_ids)
            if step < NSUB - 1:
                for i in range(lon_here):
                    cur[step + 1, s, i] = new[i]
                halos[(step + 1, s)] = send_halo(step + 1, s)
                continue
            for i in range(lon_here):
                gathered[s, 0, i] = new[i]
                levs[s, lev, i] = new[i]

            forward(s, 0)

            @pl.when(is_end)
            def _():
                raw_copy(s, 2, nlev - 1 - mate).start()
                raw_copy(s, 0, mate).start()

            @pl.when(is_inner)
            def _():
                raw_copy(s, 1, nlev - 1 - lev).start()
        if step == 0:
            lax.fori_loop(steps // 2, steps, prepare, 0)

    mix_weights(0)
    forward(0, 1)
    forward(1, 1)
    complete(0)
    search(0, 0)
    forward(0, 2)
    forward(1, 2)
    mix_weights(1)
    search(0, 1)
    for p in range(3, hops + 1):
        forward(0, p)
        forward(1, p)
    mix_weights(2)
    for group in range(1, groups - 1):
        complete(group)
        search(group, 0)
        search(group, 1)
    mix_weights(3)
    complete(groups - 1)
    wait_weights(0)
    wait_weights(1)
    search(groups - 1, 0)
    send_nums(0, 0)
    send_nums(1, 0)
    mix_levels(0)
    mix_levels(1)
    wait_weights(2)
    wait_weights(3)
    search(groups - 1, 1)
    send_nums(0, 1)
    send_nums(1, 1)

    for copy in den_copies:
        copy.wait_recv()
    den = dens[0]
    for z in range(1, nlev):
        den = den + dens[z]
    in_use = lax.broadcasted_iota(jnp.int32, (1, snd), 1) < counts[0]
    for s in range(scen):
        for part in range(2):
            for copy in num_copies[(s, part)]:
                copy.wait_recv()
            pending.extend(num_copies[(s, part)])
        num = nums[s, 0]
        for z in range(1, nlev):
            num = num + nums[s, z]
        evolved[pl.ds(s, 1), :] = jnp.where(in_use, num / den, 0.0)
    pending.extend(den_copies)
    for copy in pending:
        copy.wait_send()
    for s in range(scen):
        @pl.when(is_end)
        def _():
            mixed_copy(s).wait_recv()
            for i in range(lon_here):
                out[s, :, i, :] = mixed_in[s, i]
            raw_copy(s, 2, nlev - 1 - mate).wait_send()
            raw_copy(s, 0, mate).wait_send()

        @pl.when(is_inner)
        def _():
            raw_copy(s, 1, nlev - 1 - lev).wait_send()
            mixed_copy(s).wait_send()
    for c in range(CHUNKS):
        @pl.when(is_end)
        def _():
            weight_copy(c, 2, nlev - 1 - mate).wait_send()
            weight_copy(c, 0, mate).wait_send()

        @pl.when(is_inner)
        def _():
            weight_copy(c, 1, nlev - 1 - lev).wait_send()
            eff_copy(c).wait_send()


def body(
    tracer, u_courant, v_courant, surface_flux, mixing, kernel, column, owner_tile, offset, counts
):
    scen, lev_here, lon_here, nlat = tracer.shape
    snd = column.shape[0]
    tiles, nlev = lax.axis_size("tile"), lax.axis_size("lev")
    f32, bf16 = jnp.float32, jnp.bfloat16
    block = (lev_here, nlat)
    dma = pltpu.SemaphoreType.DMA
    vmem = pl.BlockSpec(memory_space=pltpu.VMEM)
    groups = tiles // GROUP
    out, evolved = pl.pallas_call(
        functools.partial(kernel_body, (scen, lev_here, lon_here, nlat, snd, tiles, nlev)),
        out_shape=(
            jax.ShapeDtypeStruct(tracer.shape, f32),
            jax.ShapeDtypeStruct((scen, snd), f32),
        ),
        in_specs=[vmem] * 9 + [pl.BlockSpec(memory_space=pltpu.SMEM)],
        out_specs=(vmem, vmem),
        scratch_shapes=[
            pltpu.VMEM((2, 4 * PAD, 2 * nlev * KPAD), bf16),
            pltpu.VMEM((lon_here,) + block, f32),
            pltpu.VMEM((NSUB, scen, lon_here) + block, f32),
            pltpu.VMEM((NSUB, scen) + block, f32),
            pltpu.VMEM((NSUB, scen) + block, f32),
            pltpu.VMEM(block, f32),
            pltpu.VMEM((scen, lon_here) + block, f32),
            pltpu.VMEM((scen, lon_here) + block, f32),
            pltpu.VMEM((2 * nlev * KPAD, nlat), bf16),
            pltpu.VMEM((scen, tiles, lon_here) + block, f32),
            pltpu.VMEM((scen, nlev, lon_here) + block, f32),
            pltpu.VMEM((groups, scen * GROUP * lon_here * PAD, 2 * nlat), bf16),
            pltpu.VMEM((nlat, snd), bf16),
            pltpu.VMEM((1, snd), jnp.int32),
            pltpu.VMEM((nlev, lev_here, snd), f32),
            pltpu.VMEM((lev_here, snd), f32),
            pltpu.VMEM((lev_here, snd), f32),
            pltpu.VMEM((scen, PAD, snd), f32),
            pltpu.VMEM((scen, nlev, 1, snd), f32),
            pltpu.VMEM((nlev, 1, snd), f32),
            dma((NSUB, scen, 2)),
            dma((NSUB, scen, 2)),
            dma((2,)),
            dma((scen, 4)),
            dma((scen, 4)),
            dma((CHUNKS, 4)),
            dma((CHUNKS, 4)),
            dma((scen, tiles)),
            dma((scen, tiles)),
            dma((scen, 2, nlev - 1)),
            dma((scen, 2, nlev - 1)),
            dma((nlev - 1,)),
            dma((nlev - 1,)),
        ],
        compiler_params=pltpu.CompilerParams(
            collective_id=0, has_side_effects=True, vmem_limit_bytes=56 * 2**20
        ),
    )(
        tracer,
        u_courant,
        v_courant,
        surface_flux,
        mixing,
        kernel,
        column[None],
        owner_tile[None],
        offset[None],
        counts,
    )
    return out, evolved


def solution(mesh):
    in_specs = (
        P(None, "lev", "tile", None),
        P("lev", "tile", None),
        P("lev", "tile", None),
        P(None, "tile", None),
        P(),
        P("lev", "tile"),
        P("tile"),
        P("tile"),
        P("tile"),
        P("tile"),
    )
    out_specs = (P(None, "lev", "tile", None), P(None, "tile"))
    return jax.shard_map(body, mesh=mesh, in_specs=in_specs, out_specs=out_specs, check_vma=False)
```

```python
import functools
import jax
import jax.numpy as jnp
from jax import lax
from jax.experimental import pallas as pl
from jax.experimental.pallas import tpu as pltpu
from jax.sharding import PartitionSpec as P

NSUB = 2
PAD = 24
KPAD = 32
NB = 256
CHUNKS = 4
GROUP = 4
MESH = pl.DeviceIdType.MESH


def split(x):
    high = x.astype(jnp.bfloat16)
    low = (x - high.astype(jnp.float32)).astype(jnp.bfloat16)
    return high, low


def grow(x, rows):
    return jnp.concatenate([x, jnp.zeros((rows - x.shape[0], x.shape[1]), x.dtype)], axis=0)


def flip(index, bit):
    return index + bit - 2 * bit * ((index // bit) % 2)


def substep(cells, winds, lat_winds, lat_ids):
    count = len(lat_winds)
    size = cells[0].shape[-1]
    west = [
        winds[i] * jnp.where(winds[i] > 0, cells[i], cells[i + 1]) for i in range(count + 1)
    ]
    result = []
    for i in range(count):
        centre = cells[i + 1]
        south_cells = pltpu.roll(centre, 1, 1)
        south = lat_winds[i] * jnp.where(lat_winds[i] > 0, south_cells, centre)
        south = jnp.where(lat_ids > 0, south, 0.0)
        north = pltpu.roll(south, size - 1, 1)
        result.append(centre - (west[i + 1] - west[i]) - (north - south))
    return result


def kernel_body(
    dims,
    tracer, u_in, v_in, flux, mixing, kern, column, owner, offset, counts,
    out, evolved,
    mix, u_ref, cur, halo_w, halo_e, halo_u, mixed, mixed_in, rhs, gathered, levs, lhs, onehot, lon_of,
    weight, eff, eff_out, found_at, nums, dens,
    h_send, h_recv, u_sem, z_send, z_recv, w_send, w_recv, g_send, g_recv, n_send, n_recv,
    d_send, d_recv,
):
    scen, lev_here, lon_here, nlat, snd, tiles, nlev = dims
    me, lev = lax.axis_index("tile"), lax.axis_index("lev")
    east, west = lax.rem(me + 1, tiles), lax.rem(me + tiles - 1, tiles)
    bits = [1 << k for k in range(tiles.bit_length() - 1)]
    peers = [lax.rem(lev + r, nlev) for r in range(1, nlev)]

    barrier = pltpu.get_barrier_semaphore()
    friends = [(east, lev), (west, lev)]
    friends += [(flip(me, b), lev) for b in bits]
    friends += [(me, p) for p in peers]
    for friend in friends:
        pl.semaphore_signal(barrier, inc=1, device_id=friend, device_id_type=MESH)

    row_ids = lax.broadcasted_iota(jnp.int32, (lev_here, nlat), 0)
    lat_ids = lax.broadcasted_iota(jnp.int32, (lev_here, nlat), 1)
    bottom = jnp.logical_and(row_ids == 0, lev == 0)
    for s in range(scen):
        for i in range(lon_here):
            here = tracer[s, :, i, :]
            cur[0, s, i] = jnp.where(bottom, here + flux[s, pl.ds(i, 1), :], here)
    for i in range(lon_here):
        u_ref[i] = u_in[:, i, :]
    pl.semaphore_wait(barrier, len(friends))

    def remote(src, dst, send, recv, device):
        return pltpu.make_async_remote_copy(
            src_ref=src, dst_ref=dst, send_sem=send, recv_sem=recv,
            device_id=device, device_id_type=MESH,
        )

    pending = []

    def send_halo(step, s):
        to_east = remote(
            cur.at[step, s, lon_here - 1], halo_w.at[step, s],
            h_send.at[step, s, 0], h_recv.at[step, s, 0], (east, lev),
        )
        to_west = remote(
            cur.at[step, s, 0], halo_e.at[step, s],
            h_send.at[step, s, 1], h_recv.at[step, s, 1], (west, lev),
        )
        to_east.start()
        to_west.start()
        pending.extend([to_east, to_west])
        return to_east, to_west

    u_copy = remote(u_ref.at[0], halo_u, u_sem.at[0], u_sem.at[1], (west, lev))
    u_copy.start()
    pending.append(u_copy)
    halos = {(0, s): send_halo(0, s) for s in range(scen)}

    steps = snd // NB
    half, parity = lev // 2, lev % 2
    is_end = half == parity
    is_inner = jnp.logical_not(is_end)
    mate = half * 2 + 1 - parity
    level_ids = lev * lev_here + lax.broadcasted_iota(jnp.int32, (lev_here, NB), 0)
    width = snd // CHUNKS

    def weigh(nb, carry):
        at = pl.ds(pl.multiple_of(nb * NB, NB), NB)
        used_weight = jnp.where(level_ids >= offset[:, at], kern[:, at], 0.0)
        weight[lev, :, at] = used_weight
        dens[lev, :, at] = jnp.sum(used_weight, axis=0, keepdims=True)
        return carry

    lax.fori_loop(0, steps, weigh, 0)

    def weight_copy(c, k, to):
        part = weight.at[lev, :, pl.ds(c * width, width)]
        return remote(part, part, w_send.at[c, k], w_recv.at[c, k], (me, to))

    def eff_copy(c):
        at = pl.ds(c * width, width)
        return remote(
            eff_out.at[:, at], eff.at[:, at], w_send.at[c, 3], w_recv.at[c, 3], (me, mate)
        )

    def raw_copy(s, k, to):
        return remote(
            levs.at[s, lev], levs.at[s, lev], z_send.at[s, k], z_recv.at[s, k], (me, to)
        )

    def mixed_copy(s):
        return remote(
            mixed.at[s], mixed_in.at[s], z_send.at[s, 3], z_recv.at[s, 3], (me, mate)
        )

    @pl.when(is_end)
    def _():
        for c in range(CHUNKS):
            weight_copy(c, 2, nlev - 1 - mate).start()
            weight_copy(c, 0, mate).start()

    @pl.when(is_inner)
    def _():
        for c in range(CHUNKS):
            weight_copy(c, 1, nlev - 1 - lev).start()

    den_copies = []
    for r, peer in enumerate(peers):
        copy = remote(
            dens.at[lev], dens.at[lev],
            d_send.at[r], d_recv.at[r], (me, peer),
        )
        copy.start()
        den_copies.append(copy)

    lat_rows = lax.broadcasted_iota(jnp.int32, (nlat, NB), 0)

    def prepare(nb, carry):
        at = pl.ds(pl.multiple_of(nb * NB, NB), NB)
        col = column[:, at]
        lon_in = col // nlat
        lat = col - lon_in * nlat
        onehot[:, at] = (lat_rows == lat).astype(jnp.float32).astype(jnp.bfloat16)
        lon_of[:, at] = owner[:, at] * lon_here + lon_in
        return carry

    def lay_out_mixing():
        size = nlev * lev_here
        row = lax.broadcasted_iota(jnp.int32, (4 * PAD, size), 0)
        col = lax.broadcasted_iota(jnp.int32, (4 * PAD, size), 1)
        part = sum((row >= PAD * q).astype(jnp.int32) for q in range(1, 4))
        inner = row - PAD * part
        second = (part >= 2).astype(jnp.int32)
        wanted = (half * 2 + second) * lev_here + inner
        hit = jnp.logical_and(col == wanted, inner < lev_here)
        is_low = part - 2 * second
        pick_high = jnp.where(jnp.logical_and(hit, is_low == 0), 1.0, 0.0).astype(jnp.bfloat16)
        pick_low = jnp.where(jnp.logical_and(hit, is_low == 1), 1.0, 0.0).astype(jnp.bfloat16)
        at = lax.broadcasted_iota(jnp.int32, (size, nlev * KPAD), 1)
        here = lax.broadcasted_iota(jnp.int32, (size, nlev * KPAD), 0)
        block = sum((at >= KPAD * z).astype(jnp.int32) for z in range(1, nlev))
        inner = at - KPAD * block
        hit = jnp.logical_and(here == block * lev_here + inner, inner < lev_here)
        spread = jnp.where(hit, 1.0, 0.0).astype(jnp.bfloat16)
        high, low = split(mixing[...])

        def dot(a, b, dim):
            return lax.dot_general(
                a, b, (((1,), (dim,)), ((), ())), preferred_element_type=jnp.float32
            )

        for kind in range(2):
            highs = dot(pick_high, high, kind)
            both = highs + dot(pick_low, low, kind)
            for k, rows in enumerate((both, highs)):
                placed = dot(rows.astype(jnp.bfloat16), spread, 0)
                mix[kind, :, k * nlev * KPAD:(k + 1) * nlev * KPAD] = placed.astype(jnp.bfloat16)

    def mix_blocks(kind, blocks):
        for z, block in enumerate(blocks):
            high, low = split(grow(block, KPAD))
            rhs[z * KPAD:(z + 1) * KPAD] = high
            rhs[(nlev + z) * KPAD:(nlev + z + 1) * KPAD] = low
        both = jnp.dot(mix[kind], rhs[...], preferred_element_type=jnp.float32)
        first = both[0:PAD] + both[PAD:2 * PAD]
        second = both[2 * PAD:3 * PAD] + both[3 * PAD:4 * PAD]
        own = jnp.where(parity == 0, first, second)
        other = jnp.where(parity == 0, second, first)
        return own[0:lev_here], other[0:lev_here]

    def mix_weights(c):
        @pl.when(is_inner)
        def _():
            for k in range(3):
                weight_copy(c, k, mate).wait_recv()
            for n in range(c * width, (c + 1) * width, nlat):
                at = pl.ds(n, nlat)
                own, other = mix_blocks(1, [weight[z, :, at] for z in range(nlev)])
                eff[:, at] = own
                eff_out[:, at] = other
            eff_copy(c).start()

    def wait_weights(c):
        @pl.when(is_end)
        def _():
            eff_copy(c).wait_recv()

    def mix_levels(s):
        @pl.when(is_inner)
        def _():
            for k in range(3):
                raw_copy(s, k, mate).wait_recv()
            for i in range(lon_here):
                own, other = mix_blocks(0, [levs[s, z, i] for z in range(nlev)])
                out[s, :, i, :] = own
                mixed[s, i] = other
            mixed_copy(s).start()

    orders = [bits[::-1], bits[-2:0:-1] + bits[-1:] + bits[:1]]

    def masks_at(s, p):
        held = [0]
        for bit in orders[s % 2][:p]:
            held = held + [m + bit for m in held]
        return held

    def block_copy(s, m, bit):
        return remote(
            gathered.at[s, m], gathered.at[s, m + bit],
            g_send.at[s, m + bit], g_recv.at[s, m + bit], (flip(me, bit), lev),
        )

    def forward(s, p):
        order = orders[s % 2]
        fresh = [0] if p == 0 else [m + order[p - 1] for m in masks_at(s, p - 1)]
        for m in fresh:
            if p > 0:
                block_copy(s, m - order[p - 1], order[p - 1]).wait_recv()
            for bit in order[p:]:
                copy = block_copy(s, m, bit)
                copy.start()
                pending.append(copy)

        for m in fresh:
            load_columns(s, m)

    hops = len(bits) - 1

    def arrivals(s):
        return [m + c for m in masks_at(s, hops) for c in range(2)]

    def load_columns(s, m):
        blocks = [grow(gathered[s, m, i], PAD) for i in range(lon_here)]
        high, low = split(jnp.concatenate(blocks, axis=0))
        place = arrivals(s).index(m)
        at = (s * GROUP + place % GROUP) * lon_here * PAD
        lhs[place // GROUP, at:at + lon_here * PAD, 0:nlat] = high
        lhs[place // GROUP, at:at + lon_here * PAD, nlat:2 * nlat] = low

    groups = tiles // GROUP

    num_copies = {}

    def complete(group):
        for s in range(scen):
            for m in arrivals(s)[group * GROUP:(group + 1) * GROUP]:
                if m % 2 == 1:
                    block_copy(s, m - 1, 1).wait_recv()
                    load_columns(s, m)

    def search(group, part):
        pieces = range(0, PAD, 8)

        def one_step(nb, carry):
            at = pl.ds(pl.multiple_of(nb * NB, NB), NB)
            hot = onehot[:, at]
            twice = jnp.concatenate([hot, hot], axis=0)
            lon_ids = jnp.broadcast_to(lon_of[:, at], (8, NB))
            found = jnp.dot(lhs[group], twice, preferred_element_type=jnp.float32)
            for s in range(scen):
                if group == 0:
                    acc = [jnp.zeros((8, NB), jnp.float32) for _ in pieces]
                else:
                    acc = [found_at[s, q:q + 8, at] for q in pieces]
                slots = arrivals(s)[group * GROUP:(group + 1) * GROUP]
                for inner, m in enumerate(slots):
                    tile = jnp.bitwise_xor(me, m)
                    for i in range(lon_here):
                        r = ((s * GROUP + inner) * lon_here + i) * PAD
                        here = lon_ids == tile * lon_here + i
                        acc = [
                            jnp.where(here, found[r + q:r + q + 8], old)
                            for q, old in zip(pieces, acc)
                        ]
                for q, value in zip(pieces, acc):
                    found_at[s, q:q + 8, at] = value
            return carry

        lax.fori_loop(part * steps // 2, (part + 1) * steps // 2, one_step, 0, unroll=2)

    def finish(part):
        def one_step(nb, carry):
            at = pl.ds(pl.multiple_of(nb * NB, NB), NB)
            for s in range(scen):
                terms = found_at[s, 0:lev_here, at] * eff[:, at]
                nums[s, lev, :, at] = jnp.sum(terms, axis=0, keepdims=True)
            return carry

        lax.fori_loop(part * steps // 2, (part + 1) * steps // 2, one_step, 0, unroll=2)

    def send_nums(s, part):
        at = pl.ds(part * (snd // 2), snd // 2)
        num_copies[(s, part)] = []
        for r, peer in enumerate(peers):
            copy = remote(
                nums.at[s, lev, :, at], nums.at[s, lev, :, at],
                n_send.at[s, part, r], n_recv.at[s, part, r], (me, peer),
            )
            copy.start()
            num_copies[(s, part)].append(copy)

    lay_out_mixing()
    lax.fori_loop(0, steps // 2, prepare, 0)
    u_copy.wait_recv()
    for step in range(NSUB):
        for s in range(scen):
            for copy in halos[(step, s)]:
                copy.wait_recv()
            cells = [halo_w[step, s]] + [cur[step, s, i] for i in range(lon_here)]
            cells.append(halo_e[step, s])
            winds = [u_ref[i] for i in range(lon_here)] + [halo_u[...]]
            new = substep(cells, winds, [v_in[:, i, :] for i in range(lon_here)], lat_ids)
            if step < NSUB - 1:
                for i in range(lon_here):
                    cur[step + 1, s, i] = new[i]
                halos[(step + 1, s)] = send_halo(step + 1, s)
                continue
            for i in range(lon_here):
                gathered[s, 0, i] = new[i]
                levs[s, lev, i] = new[i]

            forward(s, 0)

            @pl.when(is_end)
            def _():
                raw_copy(s, 2, nlev - 1 - mate).start()
                raw_copy(s, 0, mate).start()

            @pl.when(is_inner)
            def _():
                raw_copy(s, 1, nlev - 1 - lev).start()
        if step == 0:
            lax.fori_loop(steps // 2, steps, prepare, 0)

    mix_weights(0)
    forward(0, 1)
    forward(1, 1)
    complete(0)
    search(0, 0)
    forward(0, 2)
    forward(1, 2)
    mix_weights(1)
    search(0, 1)
    for p in range(3, hops + 1):
        forward(0, p)
        forward(1, p)
    for group in range(1, groups - 1):
        complete(group)
        search(group, 0)
        search(group, 1)
    complete(groups - 1)
    search(groups - 1, 0)
    mix_weights(2)
    mix_weights(3)
    search(groups - 1, 1)
    for part in range(2):
        for c in range(part * CHUNKS // 2, (part + 1) * CHUNKS // 2):
            wait_weights(c)
        finish(part)
        for s in range(scen):
            send_nums(s, part)
    mix_levels(0)
    mix_levels(1)

    for copy in den_copies:
        copy.wait_recv()
    den = dens[0]
    for z in range(1, nlev):
        den = den + dens[z]
    in_use = lax.broadcasted_iota(jnp.int32, (1, snd), 1) < counts[0]
    for s in range(scen):
        for part in range(2):
            for copy in num_copies[(s, part)]:
                copy.wait_recv()
            pending.extend(num_copies[(s, part)])
        num = nums[s, 0]
        for z in range(1, nlev):
            num = num + nums[s, z]
        evolved[pl.ds(s, 1), :] = jnp.where(in_use, num / den, 0.0)
    pending.extend(den_copies)
    for copy in pending:
        copy.wait_send()
    for s in range(scen):
        @pl.when(is_end)
        def _():
            mixed_copy(s).wait_recv()
            for i in range(lon_here):
                out[s, :, i, :] = mixed_in[s, i]
            raw_copy(s, 2, nlev - 1 - mate).wait_send()
            raw_copy(s, 0, mate).wait_send()

        @pl.when(is_inner)
        def _():
            raw_copy(s, 1, nlev - 1 - lev).wait_send()
            mixed_copy(s).wait_send()
    for c in range(CHUNKS):
        @pl.when(is_end)
        def _():
            weight_copy(c, 2, nlev - 1 - mate).wait_send()
            weight_copy(c, 0, mate).wait_send()

        @pl.when(is_inner)
        def _():
            weight_copy(c, 1, nlev - 1 - lev).wait_send()
            eff_copy(c).wait_send()


def body(
    tracer, u_courant, v_courant, surface_flux, mixing, kernel, column, owner_tile, offset, counts
):
    scen, lev_here, lon_here, nlat = tracer.shape
    snd = column.shape[0]
    tiles, nlev = lax.axis_size("tile"), lax.axis_size("lev")
    f32, bf16 = jnp.float32, jnp.bfloat16
    block = (lev_here, nlat)
    dma = pltpu.SemaphoreType.DMA
    vmem = pl.BlockSpec(memory_space=pltpu.VMEM)
    groups = tiles // GROUP
    out, evolved = pl.pallas_call(
        functools.partial(kernel_body, (scen, lev_here, lon_here, nlat, snd, tiles, nlev)),
        out_shape=(
            jax.ShapeDtypeStruct(tracer.shape, f32),
            jax.ShapeDtypeStruct((scen, snd), f32),
        ),
        in_specs=[vmem] * 9 + [pl.BlockSpec(memory_space=pltpu.SMEM)],
        out_specs=(vmem, vmem),
        scratch_shapes=[
            pltpu.VMEM((2, 4 * PAD, 2 * nlev * KPAD), bf16),
            pltpu.VMEM((lon_here,) + block, f32),
            pltpu.VMEM((NSUB, scen, lon_here) + block, f32),
            pltpu.VMEM((NSUB, scen) + block, f32),
            pltpu.VMEM((NSUB, scen) + block, f32),
            pltpu.VMEM(block, f32),
            pltpu.VMEM((scen, lon_here) + block, f32),
            pltpu.VMEM((scen, lon_here) + block, f32),
            pltpu.VMEM((2 * nlev * KPAD, nlat), bf16),
            pltpu.VMEM((scen, tiles, lon_here) + block, f32),
            pltpu.VMEM((scen, nlev, lon_here) + block, f32),
            pltpu.VMEM((groups, scen * GROUP * lon_here * PAD, 2 * nlat), bf16),
            pltpu.VMEM((nlat, snd), bf16),
            pltpu.VMEM((1, snd), jnp.int32),
            pltpu.VMEM((nlev, lev_here, snd), f32),
            pltpu.VMEM((lev_here, snd), f32),
            pltpu.VMEM((lev_here, snd), f32),
            pltpu.VMEM((scen, PAD, snd), f32),
            pltpu.VMEM((scen, nlev, 1, snd), f32),
            pltpu.VMEM((nlev, 1, snd), f32),
            dma((NSUB, scen, 2)),
            dma((NSUB, scen, 2)),
            dma((2,)),
            dma((scen, 4)),
            dma((scen, 4)),
            dma((CHUNKS, 4)),
            dma((CHUNKS, 4)),
            dma((scen, tiles)),
            dma((scen, tiles)),
            dma((scen, 2, nlev - 1)),
            dma((scen, 2, nlev - 1)),
            dma((nlev - 1,)),
            dma((nlev - 1,)),
        ],
        compiler_params=pltpu.CompilerParams(
            collective_id=0, has_side_effects=True, vmem_limit_bytes=56 * 2**20
        ),
    )(
        tracer,
        u_courant,
        v_courant,
        surface_flux,
        mixing,
        kernel,
        column[None],
        owner_tile[None],
        offset[None],
        counts,
    )
    return out, evolved


def solution(mesh):
    in_specs = (
        P(None, "lev", "tile", None),
        P("lev", "tile", None),
        P("lev", "tile", None),
        P(None, "tile", None),
        P(),
        P("lev", "tile"),
        P("tile"),
        P("tile"),
        P("tile"),
        P("tile"),
    )
    out_specs = (P(None, "lev", "tile", None), P(None, "tile"))
    return jax.shard_map(body, mesh=mesh, in_specs=in_specs, out_specs=out_specs, check_vma=False)
```
